512 devices in a mesh: depth: 8 (over z_lo, x), lat: 64 (over z_hi, y, core).
Axes of the slice: x: 4, y: 8, z: 8 (z_hi: 4, z_lo: 2; z = z_hi * 2 + z_lo), core: 2. Of those that a mesh axis runs over, the one named last changes fastest.
Arguments:
- fin_mask: int32 [32, 1024, 1024], P('depth', 'lat'), may hold values from 0 to 1, as said below
- stopping_power: bfloat16 [32, 1024, 1024], P('depth', 'lat'), may hold values from 0.25 to 4
- pairs_before: bfloat16 [32, 1024, 1024], P('depth', 'lat'), may hold values from 0.19921875 to 2
- clusters_before: bfloat16 [32, 1024, 1024], P('depth', 'lat'), may hold values from 0.19921875 to 2
- taps_across: bfloat16 [4, 32, 97], P(None, 'depth'), may hold values from 0 to 0.25
- taps_along: bfloat16 [4, 32, 97], P(None, 'depth'), may hold values from 0 to 0.25
- tilt_shift: int32 [32], P('depth'), may hold values from 0 to 16
- layer_doses: float32 [4, 32], P(None, 'depth'), may hold values from 0.5 to 2.5
- diffusivity: float32 [3], replicated, may hold values from 0.08 to 0.16
- reaction_rates: float32 [5], replicated, may hold values from 0.01 to 0.04
Outputs:
- concentrations: float32 [5, 32, 1024, 1024], P(None, 'depth', 'lat')
The draws below stay inside these ranges and needn't reach their ends.
Inputs may be any that keep to these rules, and one draw needn't show every extreme that they name: `fin_mask`: 1 marks silicon, 0 oxide or empty space.
All inputs are finite; a program needn't handle non-finite values.
Results may differ from the reference program's by a relative error of at most 0.00035.
Values may be sent and summed in bfloat16 or wider, within the bound.
No kernel may reach another device: no remote copies, remote signals or barrier semaphores. Data moves between devices by JAX's collectives and lax.ppermute only.
A program may use at most 64 MiB of HBM per device.

```python
import math
import jax
import jax.numpy as jnp
from jax import lax

NY = 1024
TAPS = 97
SHIFT_MAX = 16
SUBSTEPS = 2
NX = 1024
NZ = 32


def draw_fin_mask(key, part):
    key = jax.random.fold_in(key, 11)
    key_column, key_cut = jax.random.split(key)
    fin_column = jax.random.randint(key_column, (NX,), 0, 3) > 0
    gate_cut = jax.random.randint(key_cut, (NX, NY // 64), 0, 8) > 0
    top_layer = fin_column[:, None] & jnp.repeat(gate_cut, 64, axis=1)
    layer_index = jnp.arange(NZ)[:, None, None]
    silicon = jnp.where(layer_index < NZ // 2, top_layer[None, :, :], True)
    return silicon.astype(jnp.int32)


def draw_tilt_shift(key, part):
    key = jax.random.fold_in(key, 23)
    displace = jax.random.randint(key, (NZ,), 0, SHIFT_MAX + 1)
    layer_index = jnp.arange(NZ)
    displace = jnp.where(layer_index == 0, 0, displace)
    displace = jnp.where(layer_index == NZ - 1, SHIFT_MAX, displace)
    return displace.astype(jnp.int32)


def pearson_profile(key, power, norm_factor, jitter_width):
    key_tail, key_core, key_weight, key_skew, key_jitter = jax.random.split(key, 5)
    tail_width = jax.random.uniform(key_tail, (4, NZ, 1), jnp.float32, 16.0, 24.0)
    core_width = jax.random.uniform(key_core, (4, NZ, 1), jnp.float32, 1.5, 3.0)
    core_weight = jax.random.uniform(key_weight, (4, NZ, 1), jnp.float32, 0.25, 0.45)
    skewness = jax.random.uniform(key_skew, (4, NZ, 1), jnp.float32, -0.2, 0.2)
    jitter = jax.random.uniform(key_jitter, (4, NZ, TAPS), jnp.float32, 1.0 - jitter_width, 1.0 + jitter_width)
    position = (jnp.arange(TAPS) - (TAPS - 1) // 2).astype(jnp.float32)[None, None, :]
    scaled_tail = position / tail_width
    tail_part = (1.0 + 0.25 * scaled_tail * scaled_tail) ** (-power) / (norm_factor * tail_width)
    scaled_core = position / core_width
    core_part = jnp.exp(-0.5 * scaled_core * scaled_core) / (math.sqrt(2.0 * math.pi) * core_width)
    profile = core_weight * core_part + (1.0 - core_weight) * tail_part
    return profile * (1.0 + skewness * jnp.tanh(scaled_tail)) * jitter


def draw_taps_across(key, part):
    key = jax.random.fold_in(key, 31)
    return pearson_profile(key, 2.0, math.pi, 0.1).astype(jnp.bfloat16)


def draw_taps_along(key, part):
    key = jax.random.fold_in(key, 37)
    return pearson_profile(key, 2.0, math.pi, 0.1).astype(jnp.bfloat16)


def block_levels(own_key, shape, pieces, least, top_value):
    def one(dim, blocks):
        steps = jax.random.uniform(jax.random.fold_in(jax.random.fold_in(own_key, 6), dim), (blocks,), jnp.float32, least / len(pieces), top_value / len(pieces))
        return jnp.repeat(jnp.exp(steps), shape[dim] // blocks).reshape((-1,) + (1,) * (len(shape) - dim - 1))

    level = one(*pieces[0])
    for cut in pieces[1:]:
        level = level * one(*cut)
    return level


def setup_inputs(seed: int = 0) -> dict:
    seeds = jax.random.split(jax.random.key(seed), 11)
    return {
        "fin_mask": draw_fin_mask(jax.random.fold_in(seeds[10], 71), 0),
        "stopping_power": jnp.clip(jnp.exp(math.log(4.0) - 2.7725887 * jax.random.uniform(seeds[1], (NZ, NX, NY), jnp.float32) ** block_levels(seeds[1], (NZ, NX, NY), ((0, 8), (1, 64)), -0.2, 0.2)), 0.25, 4.0).astype(jnp.bfloat16),
        "pairs_before": jnp.clip(jnp.exp(math.log(2.0) - 2.306499 * jax.random.uniform(seeds[2], (NZ, NX, NY), jnp.float32) ** block_levels(seeds[2], (NZ, NX, NY), ((0, 8), (1, 64)), -0.2, 0.2)), 0.19921875, 2.0).astype(jnp.bfloat16),
        "clusters_before": jnp.clip(jnp.exp(math.log(2.0) - 2.306499 * jax.random.uniform(seeds[3], (NZ, NX, NY), jnp.float32) ** block_levels(seeds[3], (NZ, NX, NY), ((0, 8), (1, 64)), -0.2, 0.2)), 0.19921875, 2.0).astype(jnp.bfloat16),
        "taps_across": draw_taps_across(jax.random.fold_in(seeds[10], 71), 0),
        "taps_along": draw_taps_along(jax.random.fold_in(seeds[10], 71), 0),
        "tilt_shift": draw_tilt_shift(jax.random.fold_in(seeds[10], 71), 0),
        "layer_doses": jnp.clip(jnp.exp(math.log(2.5) - 1.609438 * jax.random.uniform(seeds[7], (4, NZ), jnp.float32) ** block_levels(seeds[7], (4, NZ), ((1, 8),), -0.2, 0.2)), 0.5, 2.5),
        "diffusivity": jnp.clip(jax.random.uniform(seeds[8], (3,), jnp.float32, 0.08, 0.16), 0.08, 0.16),
        "reaction_rates": jnp.clip(jax.random.uniform(seeds[9], (5,), jnp.float32, 0.01, 0.04), 0.01, 0.04),
    }


BLOCK = 128


def band_matrix(tap_values, displace):
    half_width = (tap_values.shape[0] - 1) // 2
    lead_zeros = BLOCK - half_width + SHIFT_MAX
    tail_zeros = 4 * BLOCK - (BLOCK - half_width) - tap_values.shape[0]
    band_line = jnp.concatenate([jnp.zeros((lead_zeros,), tap_values.dtype), tap_values, jnp.zeros((tail_zeros,), tap_values.dtype)])
    band_line = lax.dynamic_slice_in_dim(band_line, (SHIFT_MAX - displace).astype(jnp.int32), 4 * BLOCK)
    tiled_line = jnp.tile(band_line, BLOCK)[: BLOCK * (4 * BLOCK - 1)].reshape(BLOCK, 4 * BLOCK - 1)
    return tiled_line[:, : 3 * BLOCK]


def band_windows(values, axis):
    pad_width = [(0, 0)] * values.ndim
    pad_width[axis] = (BLOCK, BLOCK)
    padded = jnp.pad(values, pad_width)
    count = values.shape[axis] // BLOCK + 2
    shaped = padded.reshape(values.shape[:axis] + (count, BLOCK) + values.shape[axis + 1:])
    parts = [lax.slice_in_dim(shaped, start, start + count - 2, axis=axis) for start in range(3)]
    return jnp.concatenate(parts, axis=axis + 1)


def implant_layer(inputs):
    source, across, along, displace, dose = inputs
    windows_x = band_windows(source, 0).astype(jnp.float32)
    results = []
    for species in range(4):
        matrix_x = band_matrix(across[species], displace).astype(jnp.float32)
        spread = jnp.einsum("cay,ba->cby", windows_x, matrix_x).reshape(NX, NY).astype(jnp.bfloat16)
        windows_y = band_windows(spread, 1).astype(jnp.float32)
        matrix_y = band_matrix(along[species], jnp.zeros((), jnp.int32)).astype(jnp.float32)
        moved = jnp.einsum("xca,ba->xcb", windows_y, matrix_y).reshape(NX, NY)
        results.append(dose[species] * moved)
    return tuple(results)


def laplace(values):
    padded = jnp.pad(values, 1)
    near = padded[2:, 1:-1, 1:-1] + padded[:-2, 1:-1, 1:-1]
    near = near + padded[1:-1, 2:, 1:-1] + padded[1:-1, :-2, 1:-1]
    near = near + padded[1:-1, 1:-1, 2:] + padded[1:-1, 1:-1, :-2]
    return near - 6.0 * values


def reference(fin_mask, stopping_power, pairs_before, clusters_before, taps_across, taps_along, tilt_shift, layer_doses, diffusivity, reaction_rates):
    source = fin_mask.astype(jnp.bfloat16) * stopping_power
    implanted = lax.map(implant_layer, (source, jnp.transpose(taps_across, (1, 0, 2)), jnp.transpose(taps_along, (1, 0, 2)), tilt_shift, jnp.transpose(layer_doses)))
    silicon = fin_mask.astype(jnp.float32)
    arsenic = silicon * implanted[0]
    interstitial = silicon * implanted[1]
    vacancy = silicon * implanted[2]
    pair_field = silicon * pairs_before.astype(jnp.float32)
    clusters = silicon * (clusters_before.astype(jnp.float32) + implanted[3])
    for repeat in range(SUBSTEPS):
        recombine = reaction_rates[0] * interstitial * vacancy
        pairing = reaction_rates[1] * arsenic * interstitial - reaction_rates[2] * pair_field
        clustering = reaction_rates[3] * interstitial * interstitial - reaction_rates[4] * clusters
        new_inter = interstitial + silicon * (diffusivity[0] * laplace(interstitial) - recombine - pairing - 2.0 * clustering)
        new_vacancy = vacancy + silicon * (diffusivity[1] * laplace(vacancy) - recombine)
        new_arsenic = arsenic - silicon * pairing
        new_pair = pair_field + silicon * (diffusivity[2] * laplace(pair_field) + pairing)
        new_clusters = clusters + silicon * clustering
        interstitial, vacancy, arsenic, pair_field, clusters = new_inter, new_vacancy, new_arsenic, new_pair, new_clusters
    return jnp.stack([arsenic, interstitial, vacancy, pair_field, clusters])
```

```python
import jax
import jax.numpy as jnp
from jax import lax
from jax.experimental import pallas as pl
from jax.experimental.pallas import tpu as pltpu
from jax.sharding import PartitionSpec as P

TAPS = 97
HALF = 48
LAYERS = 4
ROWS = 16
LENGTH = 1024
GROUP = 24
WINDOW = 176
LATS = 64
DEPTHS = 8
F32 = jnp.float32
BF16 = jnp.bfloat16
MEMORY = 32 * 1024 * 1024


def call(kernel, outs, args, scalars=0, scratch=(), flops=1000000, size=2000000):
    specs = [pl.BlockSpec(memory_space=pltpu.SMEM)] * scalars
    specs += [pl.BlockSpec(memory_space=pltpu.VMEM)] * (len(args) - scalars)
    return pl.pallas_call(
        kernel,
        out_shape=outs,
        in_specs=specs,
        out_specs=jax.tree.map(lambda _: pl.BlockSpec(memory_space=pltpu.VMEM), outs),
        scratch_shapes=list(scratch),
        compiler_params=pltpu.CompilerParams(vmem_limit_bytes=MEMORY),
        cost_estimate=pl.CostEstimate(flops=flops, bytes_accessed=size, transcendentals=0),
    )(*args)


def shape(dims, dtype):
    return jax.ShapeDtypeStruct(dims, dtype)


def source_kernel(mask, power, pairs, clusters, packed, corner):
    sub = lax.broadcasted_iota(jnp.int32, (8, LENGTH), 0)
    edges = []
    firsts = []
    for z in range(LAYERS):
        silicon = mask[z].astype(F32)
        src = silicon * power[z].astype(F32)
        packed[pl.ds(ROWS * z, ROWS), :] = src.astype(BF16)
        pair = silicon * pairs[z].astype(F32)
        cluster = clusters[z].astype(F32)
        edge = jnp.where(sub < 2, pair[:8], jnp.where(sub >= 6, pair[8:], 0.0))
        edge = jnp.where(sub == 2, pltpu.roll(cluster[:8], 2, 0), edge)
        edge = jnp.where(sub == 5, pltpu.roll(cluster[8:], 6, 0), edge)
        edges.append(edge)
        first = jnp.where(sub < 2, src[:8], 0.0)
        firsts.append(first if z % 2 == 0 else pltpu.roll(first, 4, 0))
    packed[pl.ds(64, 16), :] = jnp.concatenate(edges[:2], 0).astype(BF16)
    packed[pl.ds(80, 16), :] = jnp.concatenate(edges[2:], 0).astype(BF16)
    corner[...] = jnp.concatenate([firsts[0] + firsts[1], firsts[2] + firsts[3]], 0).astype(BF16)


def along_matrix(line):
    wide = jnp.concatenate([line, jnp.zeros_like(line)], 1)
    wide = jnp.broadcast_to(wide, (128, 256))
    return pltpu.roll(wide, 16, 1, stride=1, stride_axis=0).astype(BF16)


def band_kernel(offset, across, along, across_bands, along_bands):
    lane = lax.broadcasted_iota(jnp.int32, (GROUP, 256), 1)
    for z in range(LAYERS):
        for s in range(4):
            line = across[pl.ds(s * LAYERS + z, 1), :]
            wide = jnp.concatenate([line, jnp.zeros_like(line)], 1)
            wide = jnp.broadcast_to(wide, (32, 256))
            band = pltpu.roll(wide, 0, 1, stride=1, stride_axis=0)
            band = pltpu.roll(band, offset[z] - 8, 1)
            group = lax.broadcasted_iota(jnp.int32, (8, 256), 0)
            last = jnp.where(group < 2, band[24:], band[:8])
            band = jnp.concatenate([band[8:24], last], 0)
            tail = pltpu.roll(band, 4 * z, 1) if z else band
            tail = jnp.where((lane >= 160 + 4 * z) & (lane < 162 + 4 * z), tail, 0.0)
            band = jnp.where(lane < 160, band, tail)
            across_bands[z, pl.ds(s * GROUP, GROUP), :] = band
            along_bands[s * LAYERS + z] = along_matrix(along[pl.ds(s * LAYERS + z, 1), :])


def pair_edge(core, z, near, mine):
    following = jnp.where(core == 0, mine[1, 0], near[1, 0])
    previous = jnp.where(core == 0, near[0, 1], mine[0, 1])
    return following, previous


def edge_of(core, z, near, mine):
    at = pl.ds(64 + 16 * (z // 2), 16)
    half = slice(8 * (z % 2), 8 * (z % 2) + 8)
    following = jnp.where(core == 0, mine[1, at, :].astype(F32), near[1, 0, at, :].astype(F32))[half]
    previous = jnp.where(core == 0, near[0, 1, at, :].astype(F32), mine[0, at, :].astype(F32))[half]
    return following, previous


def pair_edges(following, previous):
    sub = lax.broadcasted_iota(jnp.int32, (8, LENGTH), 0)
    return jnp.where(sub < 2, following, jnp.where(sub >= 6, previous, 0.0))


def cluster_edges(following, previous):
    sub = lax.broadcasted_iota(jnp.int32, (8, LENGTH), 0)
    following = pltpu.roll(following, 6, 0)
    previous = pltpu.roll(previous, 2, 0)
    return jnp.where(sub == 0, following, jnp.where(sub == 7, previous, 0.0))


def across_kernel(core_ref, mine, near, far, corner, bands, mask, pairs, clusters, lines, spread, down, up, window):
    core = core_ref[0]
    for z in range(LAYERS):
        at = pl.ds(ROWS * z, ROWS)
        parts = [far[0, 0, at, :], far[0, 1, at, :], near[0, 0, at, :], near[0, 1, at, :]]
        parts += [mine[0, at, :], mine[1, at, :]]
        parts += [near[1, 0, at, :], near[1, 1, at, :], far[1, 0, at, :], far[1, 1, at, :], corner[...]]
        for i, part in enumerate(parts):
            window[z, pl.ds(16 * i, 16), :] = part
        band = bands[z].astype(BF16)[:, :WINDOW]
        x = jnp.dot(band, window[z], preferred_element_type=F32)
        spread[z] = x.astype(BF16)
        out = down if z < 2 else up
        pair = mask[z].astype(F32) * pairs[z].astype(F32)

        def own(s):
            return x[GROUP * s : GROUP * s + ROWS].astype(BF16)

        def rim(s):
            return x[GROUP * s + ROWS : GROUP * s + GROUP]

        if z in (0, 3):
            following, previous = edge_of(core, z, near, mine)
            out[pl.ds(0, 16), :] = own(1)
            out[pl.ds(16, 16), :] = own(2)
            out[pl.ds(32, 16), :] = own(0)
            out[pl.ds(48, 16), :] = own(3)
            out[pl.ds(64, 16), :] = pair.astype(BF16)
            out[pl.ds(80, 16), :] = clusters[z]
            out[pl.ds(96, 16), :] = jnp.concatenate([rim(1), rim(2)], 0).astype(BF16)
            rows = lines[0 if z == 0 else 1].astype(F32)
            out[pl.ds(112, 16), :] = jnp.concatenate([pair_edges(following, previous), rows], 0).astype(BF16)
        else:
            out[pl.ds(128, 16), :] = own(1)
            out[pl.ds(144, 16), :] = own(2)
            out[pl.ds(160, 16), :] = pair.astype(BF16)


def along_sum(x, matrix):
    rows = x.shape[0]
    zeros = jnp.zeros((rows, 64), F32)
    wide = jnp.concatenate([zeros, x, zeros], 1)
    blocks = LENGTH // 128
    stacked = jnp.concatenate([wide[:, 128 * b : 128 * b + 256] for b in range(blocks)], 0).astype(BF16)
    y = lax.dot_general(stacked, matrix, (((1,), (1,)), ((), ())), preferred_element_type=F32)
    return jnp.concatenate([y[rows * b : rows * (b + 1)] for b in range(blocks)], 1)


def along_kernel(core_ref, doses, spread, matrices, mask, pairs, clusters, near, mine, fields):
    core = core_ref[0]
    for z in range(LAYERS):
        x = spread[z].astype(F32)
        following, previous = edge_of(core, z, near, mine)
        pair_rim = pair_edges(following, previous)
        silicon = jnp.concatenate([mask[z].astype(F32), (pair_rim > 0.0).astype(F32)], 0)
        pair = silicon * jnp.concatenate([pairs[z].astype(F32), pair_rim], 0)
        before = jnp.concatenate([clusters[z].astype(F32), cluster_edges(following, previous)], 0)
        sums = []
        for s in range(4):
            y = along_sum(x[GROUP * s : GROUP * (s + 1)], matrices[s * LAYERS + z])
            sums.append(doses[s, z] * y)
        fields[0, z] = silicon * sums[0]
        fields[1, z] = silicon * sums[1]
        fields[2, z] = silicon * sums[2]
        fields[3, z] = pair
        fields[4, z] = silicon * (before + sums[3])


def laplace(center, below, above, rows):
    total = center.shape[0]
    lane = lax.broadcasted_iota(jnp.int32, (rows, LENGTH), 1)
    inner = center[:rows]
    near = above[:rows] + below[:rows]
    near = near + pltpu.roll(center, total - 1, 0)[:rows] + pltpu.roll(center, 1, 0)[:rows]
    near = near + jnp.where(lane == LENGTH - 1, 0.0, pltpu.roll(inner, LENGTH - 1, 1))
    near = near + jnp.where(lane == 0, 0.0, pltpu.roll(inner, 1, 1))
    return near - 6.0 * inner


def react_kernel(spreads, rates, fields, below, above, result, mobile, still, late):
    for side, payload in ((0, below), (1, above)):
        near, far = (1, 0) if side == 0 else (6, 7)
        rows = payload[pl.ds(112, 16), :].astype(F32)
        pair_rim, lines = rows[:8], rows[8:]

        def implanted(i, x):
            line = lines[i : i + 1]
            dose = line[:, 128:129] + line[:, 256:257] + line[:, 384:385]
            return dose * along_sum(x, along_matrix(line[:, :128]))

        rims = payload[pl.ds(96, 16), :].astype(F32)
        pair = jnp.concatenate([payload[pl.ds(64, 16), :].astype(F32), pair_rim], 0)
        silicon = (pair > 0.0).astype(F32)
        mobile[2, near] = pair
        mobile[0, near] = silicon * implanted(0, jnp.concatenate([payload[pl.ds(0, 16), :].astype(F32), rims[:8]], 0))
        mobile[1, near] = silicon * implanted(1, jnp.concatenate([payload[pl.ds(16, 16), :].astype(F32), rims[8:]], 0))
        silicon = silicon[:ROWS]
        at = 0 if side == 0 else 5
        still[0, at, :ROWS] = silicon * implanted(2, payload[pl.ds(32, 16), :].astype(F32))
        sums = implanted(3, payload[pl.ds(48, 16), :].astype(F32))
        still[1, at, :ROWS] = silicon * (payload[pl.ds(80, 16), :].astype(F32) + sums)
        pair = payload[pl.ds(160, 16), :].astype(F32)
        silicon = (pair > 0.0).astype(F32)
        mobile[2, far, :ROWS] = pair
        mobile[0, far, :ROWS] = silicon * implanted(4, payload[pl.ds(128, 16), :].astype(F32))
        mobile[1, far, :ROWS] = silicon * implanted(5, payload[pl.ds(144, 16), :].astype(F32))
    for z in range(LAYERS):
        mobile[0, z + 2] = fields[1, z]
        mobile[1, z + 2] = fields[2, z]
        mobile[2, z + 2] = fields[3, z]
        still[0, z + 1] = fields[0, z]
        still[1, z + 1] = fields[4, z]

    def substep(silicon, centers, belows, aboves, arsenic, clusters, rows):
        inter, vacancy, pair = (c[:rows] for c in centers)
        laplaces = [laplace(c, b, a, rows) for c, b, a in zip(centers, belows, aboves)]
        recombine = rates[0] * inter * vacancy
        pairing = rates[1] * arsenic * inter - rates[2] * pair
        clustering = rates[3] * inter * inter - rates[4] * clusters
        new_inter = inter + silicon * (spreads[0] * laplaces[0] - recombine - pairing - 2.0 * clustering)
        new_vacancy = vacancy + silicon * (spreads[1] * laplaces[1] - recombine)
        new_arsenic = arsenic - silicon * pairing
        new_pair = pair + silicon * (spreads[2] * laplaces[2] + pairing)
        new_clusters = clusters + silicon * clustering
        return new_arsenic, new_inter, new_vacancy, new_pair, new_clusters

    for layer in range(1, 7):
        rows = ROWS if layer in (1, 6) else GROUP
        silicon = (mobile[2, layer, :rows] > 0.0).astype(F32)
        centers = [mobile[f, layer] for f in range(3)]
        belows = [mobile[f, layer - 1, :rows] for f in range(3)]
        aboves = [mobile[f, layer + 1, :rows] for f in range(3)]
        arsenic, clusters = still[0, layer - 1, :rows], still[1, layer - 1, :rows]
        new = substep(silicon, centers, belows, aboves, arsenic, clusters, rows)
        for f in range(3):
            late[f, layer - 1, :rows] = new[f + 1]
        still[0, layer - 1, :rows] = new[0]
        still[1, layer - 1, :rows] = new[4]
    for z in range(LAYERS):
        silicon = (mobile[2, z + 2, :ROWS] > 0.0).astype(F32)
        centers = [late[f, z + 1] for f in range(3)]
        belows = [late[f, z, :ROWS] for f in range(3)]
        aboves = [late[f, z + 2, :ROWS] for f in range(3)]
        new = substep(silicon, centers, belows, aboves, still[0, z + 1, :ROWS], still[1, z + 1, :ROWS], ROWS)
        for f in range(5):
            result[f, z] = new[f]


def moved(array, axis, size, source):
    route = [(source(i), i) for i in range(size) if source(i) is not None and 0 <= source(i) < size]
    return lax.ppermute(array, axis, route)


def lanes(core0, core1):
    return lambda i: i + core0 if i % 2 == 0 else (None if core1 is None else i + core1)


def split3(values):
    high = values.astype(BF16)
    rest = values - high.astype(F32)
    middle = rest.astype(BF16)
    return high, middle, (rest - middle.astype(F32)).astype(BF16)


def body(
    fin_mask,
    stopping_power,
    pairs_before,
    clusters_before,
    taps_across,
    taps_along,
    tilt_shift,
    layer_doses,
    diffusivity,
    reaction_rates,
):
    core = lax.rem(lax.axis_index("lat"), 2)
    core_ref = core.reshape(1)
    couples = [[2 * i, 2 * i + 1] for i in range(LATS // 2)]

    packed, first = call(
        source_kernel,
        (shape((96, LENGTH), BF16), shape((16, LENGTH), BF16)),
        (fin_mask, stopping_power, pairs_before, clusters_before),
    )
    corner = moved(first, "lat", LATS, lambda i: None if i % 2 == 0 else i + 5)
    mine = lax.all_gather(packed, "lat", axis_index_groups=couples)
    near = moved(mine, "lat", LATS, lanes(-2, 2))
    far = moved(mine[:, :64], "lat", LATS, lanes(-4, 4))

    wide = ((0, 0), (0, 0), (0, 128 - TAPS))
    across = jnp.pad(taps_across.astype(F32), wide).reshape(16, 128)
    along_taps = jnp.pad(taps_along, wide)
    along = along_taps.astype(F32).reshape(16, 128)
    offset = ROWS + ROWS * core + tilt_shift
    across_bands, along_bands = call(
        band_kernel,
        (shape((LAYERS, 4 * GROUP, 256), F32), shape((16, 128, 256), BF16)),
        (offset, across, along),
        scalars=1,
    )
    pieces = [along_taps] + [jnp.broadcast_to(d[:, :, None], (4, LAYERS, 128)) for d in split3(layer_doses)]
    table = jnp.concatenate(pieces, 2)
    order = ((1, 0), (2, 0), (0, 0), (3, 0), (1, 1), (2, 1), (1, 1), (2, 1))
    lines = jnp.stack(
        [
            jnp.stack([table[s, far_layer] for s, far_layer in order]),
            jnp.stack([table[s, 3 - far_layer] for s, far_layer in order]),
        ]
    )
    lines = jnp.pad(lines, ((0, 0), (0, 0), (0, 512)))

    near = lax.all_gather(near, "lat", axis_index_groups=couples)
    far = lax.all_gather(far, "lat", axis_index_groups=couples)
    spread, down, up = call(
        across_kernel,
        (shape((LAYERS, 4 * GROUP, LENGTH), BF16), shape((176, LENGTH), BF16), shape((176, LENGTH), BF16)),
        (core_ref, mine, near, far, corner, across_bands, fin_mask, pairs_before, clusters_before, lines),
        scalars=1,
        scratch=[pltpu.VMEM((LAYERS, WINDOW, LENGTH), BF16)],
    )
    below = moved(up, "depth", DEPTHS, lambda i: i - 1)
    above = moved(down, "depth", DEPTHS, lambda i: i + 1)
    fields = call(
        along_kernel,
        shape((5, LAYERS, GROUP, LENGTH), F32),
        (core_ref, layer_doses, spread, along_bands, fin_mask, pairs_before, clusters_before, near, mine),
        scalars=2,
    )
    return call(
        react_kernel,
        shape((5, LAYERS, ROWS, LENGTH), F32),
        (diffusivity, reaction_rates, fields, below, above),
        scalars=2,
        scratch=[
            pltpu.VMEM((3, 8, GROUP, LENGTH), F32),
            pltpu.VMEM((2, 6, GROUP, LENGTH), F32),
            pltpu.VMEM((3, 6, GROUP, LENGTH), F32),
        ],
    )


def solution(mesh):
    return jax.shard_map(
        body,
        mesh=mesh,
        in_specs=(
            P("depth", "lat", None),
            P("depth", "lat", None),
            P("depth", "lat", None),
            P("depth", "lat", None),
            P(None, "depth", None),
            P(None, "depth", None),
            P("depth"),
            P(None, "depth"),
            P(),
            P(),
        ),
        out_specs=P(None, "depth", "lat", None),
        check_vma=False,
    )
```

```python
import functools

import jax
import jax.numpy as jnp
from jax import lax
from jax.experimental import pallas as pl
from jax.experimental.pallas import tpu as pltpu
from jax.sharding import PartitionSpec as P

TAPS = 97
HALF = 48
LAYERS = 4
ROWS = 16
LENGTH = 1024
GROUP = 24
WINDOW = 176
LATS = 64
DEPTHS = 8
F32 = jnp.float32
BF16 = jnp.bfloat16
MEMORY = 32 * 1024 * 1024


def call(kernel, outs, args, scalars=0, hbm=(), hbm_out=False, scratch=(), aliases={}, flops=1000000, size=2000000):
    def space(i):
        return pltpu.SMEM if i < scalars else pltpu.HBM if i in hbm else pltpu.VMEM

    out_space = pltpu.HBM if hbm_out else pltpu.VMEM
    return pl.pallas_call(
        kernel,
        out_shape=outs,
        in_specs=[pl.BlockSpec(memory_space=space(i)) for i in range(len(args))],
        out_specs=jax.tree.map(lambda _: pl.BlockSpec(memory_space=out_space), outs),
        scratch_shapes=list(scratch),
        input_output_aliases=aliases,
        compiler_params=pltpu.CompilerParams(vmem_limit_bytes=MEMORY),
        cost_estimate=pl.CostEstimate(flops=flops, bytes_accessed=size, transcendentals=0),
    )(*args)


def shape(dims, dtype):
    return jax.ShapeDtypeStruct(dims, dtype)


def tile(z):
    return pl.ds(ROWS * z, ROWS)


def along_matrix(line):
    wide = jnp.concatenate([line, jnp.zeros_like(line)], 1)
    wide = jnp.broadcast_to(wide, (128, 256))
    return pltpu.roll(wide, 16, 1, stride=1, stride_axis=0).astype(BF16)


def own_core():
    return lax.rem(lax.axis_index("lat"), 2)


def wide_taps(taps, lines):
    lines[...] = jnp.zeros_like(lines)
    for s in range(4):
        lines[pl.ds(s * LAYERS, LAYERS), :TAPS] = taps[s].astype(F32)


def band_kernel(tilt, taps_across, across_bands, across):
    wide_taps(taps_across, across)
    lane = lax.broadcasted_iota(jnp.int32, (GROUP, 256), 1)
    group = lax.broadcasted_iota(jnp.int32, (8, 256), 0)
    for z in range(LAYERS):
        offset = ROWS - 8 + ROWS * own_core() + tilt[z]
        for s in range(4):
            line = across[pl.ds(s * LAYERS + z, 1), :]
            wide = jnp.concatenate([line, jnp.zeros_like(line)], 1)
            wide = jnp.broadcast_to(wide, (32, 256))
            band = pltpu.roll(wide, 0, 1, stride=1, stride_axis=0)
            band = pltpu.roll(band, offset, 1)
            last = jnp.where(group < 2, band[24:], band[:8])
            band = jnp.concatenate([band[8:24], last], 0)
            tail = pltpu.roll(band, 4 * z, 1) if z else band
            tail = jnp.where((lane >= 160 + 4 * z) & (lane < 162 + 4 * z), tail, 0.0)
            across_bands[z, pl.ds(s * GROUP, GROUP), :] = jnp.where(lane < 160, band, tail)


def pair_edges(following, previous):
    sub = lax.broadcasted_iota(jnp.int32, (8, LENGTH), 0)
    return jnp.where(sub < 2, following, jnp.where(sub >= 6, previous, 0.0))


def cluster_edges(following, previous):
    sub = lax.broadcasted_iota(jnp.int32, (8, LENGTH), 0)
    following = pltpu.roll(following, 6, 0)
    previous = pltpu.roll(previous, 2, 0)
    return jnp.where(sub == 0, following, jnp.where(sub == 7, previous, 0.0))


SENT = ((1, 0), (2, 0), (0, 0), (3, 0), (1, 1), (2, 1))


def early_kernel(doses, pair, clusters, taps_along, down, up, taps, lines):
    wide_taps(taps_along, taps)
    lines[...] = jnp.zeros_like(lines)
    for side, (out, near, far) in enumerate(((down, 0, 1), (up, 3, 2))):
        for i, (s, distance) in enumerate(SENT):
            z = far if distance else near
            row = pl.ds(16 * side + 8 + i, 1)
            lines[row, pl.ds(0, 128)] = taps[pl.ds(s * LAYERS + z, 1), :]
            dose = jnp.full((1, 128), doses[s, z], F32)
            for part in range(1, 4):
                rounded = dose.astype(BF16).astype(F32)
                lines[row, pl.ds(128 * part, 128)] = rounded
                dose = dose - rounded
        out[pl.ds(0, 16), :] = pair[tile(near), :]
        out[pl.ds(16, 16), :] = clusters[near]
        out[pl.ds(32, 16), :] = pair[tile(far), :]
        out[pl.ds(48, 16), :] = lines[pl.ds(16 * side, 16), :].astype(BF16)


def across_kernel(
    mine, near, far, corner, bands, edges, others, early_down, early_up, spread, down, up, rims, window
):
    core = own_core()
    for out, early in ((down, early_down), (up, early_up)):
        out[pl.ds(112, 48), :] = early[pl.ds(0, 48), :]
    for z in range(LAYERS):
        at, also = tile(z), pl.ds(64 + ROWS * z, ROWS)
        parts = [far[0, at, :], far[0, also, :], near[0, at, :], near[0, also, :]]
        parts += [mine[0, at, :], mine[1, at, :], near[1, at, :], near[1, also, :]]
        parts += [far[1, at, :], far[1, also, :], corner[...]]
        for i, part in enumerate(parts):
            window[z, pl.ds(16 * i, 16), :] = part
        x = jnp.dot(bands[z].astype(BF16)[:, :WINDOW], window[z], preferred_element_type=F32)
        spread[z] = x.astype(BF16)
        half = slice(8 * (z % 2), 8 * (z % 2) + 8)
        at = pl.ds(16 * (z // 2), 16)
        other = others[at, :].astype(F32)
        following = jnp.where(core == 0, edges[1, at, :].astype(F32), other)[half]
        previous = jnp.where(core == 0, other, edges[0, at, :].astype(F32))[half]
        rims[0, z] = pair_edges(following, previous)
        rims[1, z] = cluster_edges(following, previous)
        out = down if z < 2 else up
        own = [x[GROUP * s : GROUP * s + ROWS].astype(BF16) for s in range(4)]
        rim = [x[GROUP * s + ROWS : GROUP * s + GROUP] for s in range(4)]
        if z in (0, 3):
            for i, s in enumerate((1, 2, 0, 3)):
                out[pl.ds(16 * i, 16), :] = own[s]
            out[pl.ds(64, 16), :] = jnp.concatenate([rim[1], rim[2]], 0).astype(BF16)
            lines = (early_down if z < 2 else early_up)[pl.ds(48, 16), :].astype(F32)[8:]
            out[pl.ds(160, 16), :] = jnp.concatenate([rims[0, z], lines], 0).astype(BF16)
        else:
            out[pl.ds(80, 16), :] = own[1]
            out[pl.ds(96, 16), :] = own[2]


def along_sum(x, matrix):
    rows = x.shape[0]
    zeros = jnp.zeros((rows, 64), F32)
    wide = jnp.concatenate([zeros, x, zeros], 1)
    blocks = LENGTH // 128
    stacked = jnp.concatenate([wide[:, 128 * b : 128 * b + 256] for b in range(blocks)], 0).astype(BF16)
    y = lax.dot_general(stacked, matrix, (((1,), (1,)), ((), ())), preferred_element_type=F32)
    return jnp.concatenate([y[rows * b : rows * (b + 1)] for b in range(blocks)], 1)


def laplace(center, below, above, rows):
    total = center.shape[0]
    inner = center[:rows]
    lane = lax.broadcasted_iota(jnp.int32, (rows, 128), 1)
    right = pltpu.roll(inner, LENGTH - 1, 1)
    left = pltpu.roll(inner, 1, 1)
    right = jnp.concatenate([right[:, :-128], jnp.where(lane == 127, 0.0, right[:, -128:])], 1)
    left = jnp.concatenate([jnp.where(lane == 0, 0.0, left[:, :128]), left[:, 128:]], 1)
    near = right + left
    near = near + pltpu.roll(center, total - 1, 0)[:rows] + pltpu.roll(center, 1, 0)[:rows]
    for layer in (below, above):
        if layer is not None:
            near = near + layer[:rows]
    return near - 6.0 * inner


def substep(spreads, rates, silicon, centers, belows, aboves, arsenic, clusters, rows):
    inter, vacancy, pair = (c[:rows] for c in centers)
    flows = [
        silicon * (spreads[f] * laplace(centers[f], belows[f], aboves[f], rows)) for f in range(3)
    ]
    recombine = rates[0] * inter * vacancy
    pairing = rates[1] * arsenic * inter - rates[2] * pair
    clustering = rates[3] * inter * inter - rates[4] * clusters
    new_inter = inter + (flows[0] - recombine - pairing - 2.0 * clustering)
    new_vacancy = vacancy + (flows[1] - recombine)
    new_pair = pair + (flows[2] + pairing)
    return (new_inter, new_vacancy, new_pair), (arsenic - pairing, clusters + clustering)


NONE = (None, None, None)


def along_kernel(spreads, rates, doses, spread, taps_along, pairs, clusters, rims, outer, late, still, fields, fixed, along):
    wide_taps(taps_along, along)
    for z in range(LAYERS):
        x = spread[z].astype(F32)
        pair = jnp.concatenate([pairs[tile(z), :].astype(F32), rims[0, z]], 0)
        silicon = (pair > 0.0).astype(F32)
        before = jnp.concatenate([clusters[z].astype(F32), rims[1, z]], 0)
        sums = []
        for s in range(4):
            matrix = along_matrix(along[pl.ds(s * LAYERS + z, 1), :])
            y = along_sum(x[GROUP * s : GROUP * (s + 1)], matrix)
            sums.append(doses[s, z] * y)
        fields[0, z] = silicon * sums[1]
        fields[1, z] = silicon * sums[2]
        fields[2, z] = pair
        fixed[0, z] = silicon * sums[0]
        fixed[1, z] = silicon * (before + sums[3])
    for z in range(LAYERS):
        silicon = (fields[2, z] > 0.0).astype(F32)
        belows = [fields[f, z - 1] for f in range(3)] if z > 0 else NONE
        aboves = [fields[f, z + 1] for f in range(3)] if z < LAYERS - 1 else NONE
        centers = [fields[f, z] for f in range(3)]
        mobile, others = substep(spreads, rates, silicon, centers, belows, aboves, fixed[0, z], fixed[1, z], GROUP)
        for f in range(3):
            late[f, z] = mobile[f]
            if z in (0, 3):
                outer[f, z // 3] = fields[f, z, :ROWS]
        for f in range(2):
            still[f, z] = others[f][:ROWS]


def react_kernel(side, spreads, rates, outer, late, still, pairs, rims_own, payload, *refs):
    result, near_late, own_late, done, sems = refs[-5:]

    def sent(i):
        return payload[pl.ds(16 * i, 16), :].astype(F32)

    rows = sent(10)
    pair_rim, lines = rows[:8], rows[8:]

    def implanted(i, x):
        line = lines[i : i + 1]
        dose = line[:, 128:129] + line[:, 256:257] + line[:, 384:385]
        return dose * along_sum(x, along_matrix(line[:, :128]))

    rims = sent(4)
    pair = jnp.concatenate([sent(7), pair_rim], 0)
    silicon = (pair > 0.0).astype(F32)
    near = [
        silicon * implanted(0, jnp.concatenate([sent(0), rims[:8]], 0)),
        silicon * implanted(1, jnp.concatenate([sent(1), rims[8:]], 0)),
        pair,
    ]
    silicon = silicon[:ROWS]
    arsenic = silicon * implanted(2, sent(2))
    clusters = silicon * (sent(8) + implanted(3, sent(3)))
    far_pair = sent(9)
    far_silicon = (far_pair > 0.0).astype(F32)
    far = [far_silicon * implanted(4, sent(5)), far_silicon * implanted(5, sent(6)), far_pair]
    beside = [outer[f, side] for f in range(3)]
    mobile, _ = substep(spreads, rates, silicon, near, far, beside, arsenic, clusters, ROWS)
    z = 3 * side
    own_pair = jnp.concatenate([pairs[tile(z), :].astype(F32), rims_own[0, z]], 0)
    own_silicon = (own_pair > 0.0).astype(F32)
    for f in range(3):
        near_late[f] = mobile[f]
        own_late[f] = late[f, z] + own_silicon * (spreads[f] * near[f])

    def layer(f, at):
        if at in (-1, LAYERS):
            return near_late[f]
        return own_late[f] if at == z else late[f, at]

    for i in range(2):
        at = 2 * side + i
        silicon = (pairs[tile(at), :].astype(F32) > 0.0).astype(F32)
        centers = [layer(f, at) for f in range(3)]
        belows = [layer(f, at - 1) for f in range(3)]
        aboves = [layer(f, at + 1) for f in range(3)]
        mobile, others = substep(spreads, rates, silicon, centers, belows, aboves, still[0, at], still[1, at], ROWS)
        for f, new in enumerate((others[0], *mobile, others[1])):
            done[f, i] = new
        pltpu.make_async_copy(done.at[:, i], result.at[:, at], sems.at[i]).start()
    for i in range(2):
        pltpu.make_async_copy(done.at[:, i], result.at[:, 2 * side + i], sems.at[i]).wait()


def moved(array, axis, size, source):
    route = [(source(i), i) for i in range(size) if source(i) is not None and 0 <= source(i) < size]
    return lax.ppermute(array, axis, route)


def lanes(core0, core1):
    return lambda i: i + core0 if i % 2 == 0 else (None if core1 is None else i + core1)


def body(
    fin_mask,
    stopping_power,
    pairs_before,
    clusters_before,
    taps_across,
    taps_along,
    tilt_shift,
    layer_doses,
    diffusivity,
    reaction_rates,
):
    couples = [[2 * i, 2 * i + 1] for i in range(LATS // 2)]

    def shared(array):
        return lax.all_gather(array, "lat", axis_index_groups=couples)

    silicon = fin_mask.astype(BF16)
    source = silicon * stopping_power
    pair = silicon * pairs_before
    edges = [pair[:, :2], clusters_before[:, :1], pair[:, 3:5], clusters_before[:, 15:], pair[:, 14:]]
    edges = jnp.concatenate(edges, 1).reshape(32, LENGTH)
    others = moved(edges, "lat", LATS, lanes(-1, 1))
    pair = pair.reshape(64, LENGTH)
    mine = shared(source.reshape(64, LENGTH)).reshape(128, LENGTH)
    near = moved(mine, "lat", LATS, lanes(-2, 2))
    far = moved(mine, "lat", LATS, lanes(-4, 4))
    corner = jnp.pad(source[:, :2], ((0, 0), (0, 2), (0, 0))).reshape(16, LENGTH)
    corner = moved(corner, "lat", LATS, lambda i: None if i % 2 == 0 else i + 5)
    edges, corner = lax.optimization_barrier((edges, corner))
    edges = shared(edges)
    early_down, early_up = call(
        early_kernel,
        (shape((64, LENGTH), BF16), shape((64, LENGTH), BF16)),
        (layer_doses, pair, clusters_before, taps_along),
        scalars=1,
        scratch=[pltpu.VMEM((16, 128), F32), pltpu.VMEM((32, LENGTH), F32)],
    )
    across_bands = call(
        band_kernel,
        shape((LAYERS, 4 * GROUP, 256), F32),
        (tilt_shift, taps_across),
        scalars=1,
        scratch=[pltpu.VMEM((16, 128), F32)],
    )
    near = shared(near)
    far, near, early_down, early_up = lax.optimization_barrier((far, near, early_down, early_up))
    far = shared(far)
    others, far = lax.optimization_barrier((others, far))
    spread, down, up, rims = call(
        across_kernel,
        (
            shape((LAYERS, 4 * GROUP, LENGTH), BF16),
            shape((176, LENGTH), BF16),
            shape((176, LENGTH), BF16),
            shape((2, LAYERS, 8, LENGTH), F32),
        ),
        (
            mine.reshape(2, 64, LENGTH),
            near.reshape(2, 128, LENGTH),
            far,
            corner,
            across_bands,
            edges,
            others,
            early_down,
            early_up,
        ),
        scratch=[pltpu.VMEM((LAYERS, WINDOW, LENGTH), BF16)],
    )
    below = moved(up, "depth", DEPTHS, lambda i: i - 1)
    above = moved(down, "depth", DEPTHS, lambda i: i + 1)
    outer, late, still = call(
        along_kernel,
        (
            shape((3, 2, ROWS, LENGTH), F32),
            shape((3, LAYERS, GROUP, LENGTH), F32),
            shape((2, LAYERS, ROWS, LENGTH), F32),
        ),
        (diffusivity, reaction_rates, layer_doses, spread, taps_along, pair, clusters_before, rims),
        scalars=3,
        scratch=[
            pltpu.VMEM((3, LAYERS, GROUP, LENGTH), F32),
            pltpu.VMEM((2, LAYERS, GROUP, LENGTH), F32),
            pltpu.VMEM((16, 128), F32),
        ],
    )
    scratch = [
        pltpu.VMEM((3, ROWS, LENGTH), F32),
        pltpu.VMEM((3, GROUP, LENGTH), F32),
        pltpu.VMEM((5, 2, ROWS, LENGTH), F32),
        pltpu.SemaphoreType.DMA((2,)),
    ]
    given = (diffusivity, reaction_rates, outer, late, still, pair, rims)
    for side, payload in enumerate((below, above)):
        args = (*given, payload) if side == 0 else (*given, payload, result)
        result = call(
            functools.partial(react_kernel, side),
            shape((5, LAYERS, ROWS, LENGTH), F32),
            args,
            scalars=2,
            hbm=(8,),
            hbm_out=True,
            scratch=scratch,
            aliases={8: 0} if side else {},
        )
    return result


def solution(mesh):
    return jax.shard_map(
        body,
        mesh=mesh,
        in_specs=(
            P("depth", "lat", None),
            P("depth", "lat", None),
            P("depth", "lat", None),
            P("depth", "lat", None),
            P(None, "depth", None),
            P(None, "depth", None),
            P("depth"),
            P(None, "depth"),
            P(),
            P(),
        ),
        out_specs=P(None, "depth", "lat", None),
        check_vma=False,
    )
```

```python
import functools

import jax
import jax.numpy as jnp
from jax import lax
from jax.experimental import pallas as pl
from jax.experimental.pallas import tpu as pltpu
from jax.sharding import PartitionSpec as P

TAPS = 97
HALF = 48
LAYERS = 4
ROWS = 16
LENGTH = 1024
GROUP = 24
WINDOW = 176
LATS = 64
DEPTHS = 8
F32 = jnp.float32
BF16 = jnp.bfloat16
MEMORY = 32 * 1024 * 1024


def call(kernel, outs, args, scalars=0, hbm=(), hbm_out=False, scratch=(), aliases={}, flops=1000000, size=2000000):
    def space(i):
        return pltpu.SMEM if i < scalars else pltpu.HBM if i in hbm else pltpu.VMEM

    out_space = pltpu.HBM if hbm_out else pltpu.VMEM
    return pl.pallas_call(
        kernel,
        out_shape=outs,
        in_specs=[pl.BlockSpec(memory_space=space(i)) for i in range(len(args))],
        out_specs=jax.tree.map(lambda _: pl.BlockSpec(memory_space=out_space), outs),
        scratch_shapes=list(scratch),
        input_output_aliases=aliases,
        compiler_params=pltpu.CompilerParams(vmem_limit_bytes=MEMORY),
        cost_estimate=pl.CostEstimate(flops=flops, bytes_accessed=size, transcendentals=0),
    )(*args)


def shape(dims, dtype):
    return jax.ShapeDtypeStruct(dims, dtype)


def tile(z):
    return pl.ds(ROWS * z, ROWS)


def along_matrix(line):
    wide = jnp.concatenate([line, jnp.zeros_like(line)], 1)
    wide = jnp.broadcast_to(wide, (128, 256))
    return pltpu.roll(wide, 16, 1, stride=1, stride_axis=0).astype(BF16)


def own_core():
    return lax.rem(lax.axis_index("lat"), 2)


def wide_taps(taps, lines):
    lines[...] = jnp.zeros_like(lines)
    for s in range(4):
        lines[pl.ds(s * LAYERS, LAYERS), :TAPS] = taps[s].astype(F32)


def pair_edges(following, previous):
    sub = lax.broadcasted_iota(jnp.int32, (8, LENGTH), 0)
    return jnp.where(sub < 2, following, jnp.where(sub >= 6, previous, 0.0))


def cluster_edges(following, previous):
    sub = lax.broadcasted_iota(jnp.int32, (8, LENGTH), 0)
    following = pltpu.roll(following, 6, 0)
    previous = pltpu.roll(previous, 2, 0)
    return jnp.where(sub == 0, following, jnp.where(sub == 7, previous, 0.0))


SENT = ((1, 0), (2, 0), (0, 0), (3, 0), (1, 1), (2, 1))


def prepare_kernel(tilt, doses, taps_across, taps_along, pair, clusters, across_bands, down, up, across, taps, lines):
    wide_taps(taps_across, across)
    lane = lax.broadcasted_iota(jnp.int32, (GROUP, 256), 1)
    group = lax.broadcasted_iota(jnp.int32, (8, 256), 0)
    for z in range(LAYERS):
        offset = ROWS - 8 + ROWS * own_core() + tilt[z]
        for s in range(4):
            line = across[pl.ds(s * LAYERS + z, 1), :]
            wide = jnp.concatenate([line, jnp.zeros_like(line)], 1)
            wide = pltpu.roll(jnp.broadcast_to(wide, (8, 256)), offset, 1)
            band = pltpu.roll(jnp.broadcast_to(wide[:1], (32, 256)), 0, 1, stride=1, stride_axis=0)
            last = jnp.where(group < 2, band[24:], band[:8])
            band = jnp.concatenate([band[8:24], last], 0)
            tail = pltpu.roll(band, 4 * z, 1) if z else band
            tail = jnp.where((lane >= 160 + 4 * z) & (lane < 162 + 4 * z), tail, 0.0)
            across_bands[z, pl.ds(s * GROUP, GROUP), :] = jnp.where(lane < 160, band, tail)
    wide_taps(taps_along, taps)
    lines[...] = jnp.zeros_like(lines)
    for side, (out, near, far) in enumerate(((down, 0, 1), (up, 3, 2))):
        for i, (s, distance) in enumerate(SENT):
            z = far if distance else near
            row = pl.ds(16 * side + 8 + i, 1)
            lines[row, pl.ds(0, 128)] = taps[pl.ds(s * LAYERS + z, 1), :]
            dose = jnp.full((1, 128), doses[s, z], F32)
            for part in range(1, 4):
                rounded = dose.astype(BF16).astype(F32)
                lines[row, pl.ds(128 * part, 128)] = rounded
                dose = dose - rounded
        out[pl.ds(0, 16), :] = pair[tile(near), :]
        out[pl.ds(16, 16), :] = clusters[near]
        out[pl.ds(32, 16), :] = pair[tile(far), :]
        out[pl.ds(48, 16), :] = lines[pl.ds(16 * side, 16), :].astype(BF16)


def packed_rims(fields):
    sub = lax.broadcasted_iota(jnp.int32, (8, LENGTH), 0)
    total = jnp.where((sub == 0) | (sub == 7), fields[0], 0.0)
    for i, field in enumerate(fields[1:], 1):
        total = jnp.where(sub == i, pltpu.roll(field, i, 0), total)
        total = jnp.where(sub == 7 - i, pltpu.roll(field, 8 - i, 0), total)
    return total


def unpacked_rim(packed, i):
    sub = lax.broadcasted_iota(jnp.int32, (8, LENGTH), 0)
    following = pltpu.roll(packed, 8 - i, 0) if i else packed
    previous = pltpu.roll(packed, i, 0) if i else packed
    return jnp.where(sub == 0, following, jnp.where(sub == 7, previous, 0.0))


def across_kernel(
    mine, near, received, far, corner, bands, early_down, early_up, spread, across_even, across_odd, rims, window
):
    core = own_core()
    payloads = ({}, {})
    for payload, early in zip(payloads, (early_down, early_up)):
        payload[112, 48] = early[pl.ds(0, 48), :]
    for z in range(LAYERS):
        at, also = tile(z), pl.ds(64 + ROWS * z, ROWS)
        parts = [far[0, at, :], far[0, also, :], near[0, at, :], near[0, also, :]]
        parts += [mine[0, at, :], mine[1, at, :], near[1, at, :], near[1, also, :]]
        parts += [far[1, at, :], far[1, also, :], corner[...]]
        for i, part in enumerate(parts):
            window[z, pl.ds(16 * i, 16), :] = part
        x = jnp.dot(bands[z].astype(BF16)[:, :WINDOW], window[z], preferred_element_type=F32)
        spread[z] = x.astype(BF16)
        half = slice(8 * (z // 2), 8 * (z // 2) + 8)
        at = pl.ds(128, 16)
        other = received[at, :].astype(F32)
        following = jnp.where(core == 0, near[1, at, :].astype(F32), other)[half]
        previous = jnp.where(core == 0, other, near[0, at, :].astype(F32))[half]
        if z % 2:
            following = pltpu.roll(following, 4, 0)
        else:
            previous = pltpu.roll(previous, 4, 0)
        rims[0, z] = pair_edges(following, previous)
        rims[1, z] = cluster_edges(following, previous)
        payload = payloads[z // 2]
        own = [x[GROUP * s : GROUP * s + ROWS].astype(BF16) for s in range(4)]
        rim = [x[GROUP * s + ROWS : GROUP * s + GROUP] for s in range(4)]
        if z in (0, 3):
            for i, s in enumerate((1, 2, 0, 3)):
                payload[16 * i, 16] = own[s]
            lines = (early_down if z < 2 else early_up)[pl.ds(48, 16), :].astype(F32)[8:]
            packed = packed_rims((rim[1], rim[2], rims[0, z]))
            payload[64, 16] = jnp.concatenate([packed, lines], 0).astype(BF16)
        else:
            payload[80, 16] = own[1]
            payload[96, 16] = own[2]

    def write(payload, out):
        for (start, size), value in payload.items():
            out[pl.ds(start, size), :] = value

    odd = lax.rem(lax.axis_index("depth"), 2)

    @pl.when(odd == 0)
    def _():
        write(payloads[0], across_odd)
        write(payloads[1], across_even)

    @pl.when(odd == 1)
    def _():
        write(payloads[0], across_even)
        write(payloads[1], across_odd)


def along_sum(x, matrix):
    rows = x.shape[0]
    zeros = jnp.zeros((rows, 64), F32)
    wide = jnp.concatenate([zeros, x, zeros], 1)
    blocks = LENGTH // 128
    stacked = jnp.concatenate([wide[:, 128 * b : 128 * b + 256] for b in range(blocks)], 0).astype(BF16)
    y = lax.dot_general(stacked, matrix, (((1,), (1,)), ((), ())), preferred_element_type=F32)
    return jnp.concatenate([y[rows * b : rows * (b + 1)] for b in range(blocks)], 1)


def laplace(center, below, above, rows):
    total = center.shape[0]
    inner = center[:rows]
    lane = lax.broadcasted_iota(jnp.int32, (rows, 128), 1)
    right = pltpu.roll(inner, LENGTH - 1, 1)
    left = pltpu.roll(inner, 1, 1)
    right = jnp.concatenate([right[:, :-128], jnp.where(lane == 127, 0.0, right[:, -128:])], 1)
    left = jnp.concatenate([jnp.where(lane == 0, 0.0, left[:, :128]), left[:, 128:]], 1)
    near = right + left
    near = near + pltpu.roll(center, total - 1, 0)[:rows] + pltpu.roll(center, 1, 0)[:rows]
    for layer in (below, above):
        if layer is not None:
            near = near + layer[:rows]
    return near - 6.0 * inner


def substep(spreads, rates, silicon, centers, belows, aboves, arsenic, clusters, rows):
    inter, vacancy, pair = (c[:rows] for c in centers)
    flows = [
        silicon * (spreads[f] * laplace(centers[f], belows[f], aboves[f], rows)) for f in range(3)
    ]
    recombine = rates[0] * inter * vacancy
    pairing = rates[1] * arsenic * inter - rates[2] * pair
    clustering = rates[3] * inter * inter - rates[4] * clusters
    new_inter = inter + (flows[0] - recombine - pairing - 2.0 * clustering)
    new_vacancy = vacancy + (flows[1] - recombine)
    new_pair = pair + (flows[2] + pairing)
    return (new_inter, new_vacancy, new_pair), (arsenic - pairing, clusters + clustering)


NONE = (None, None, None)


def along_kernel(spreads, rates, doses, spread, taps_along, pairs, clusters, rims, outer, late, still, fields, fixed, along):
    wide_taps(taps_along, along)
    for z in range(LAYERS):
        x = spread[z].astype(F32)
        pair = jnp.concatenate([pairs[tile(z), :].astype(F32), rims[0, z]], 0)
        silicon = (pair > 0.0).astype(F32)
        before = jnp.concatenate([clusters[z].astype(F32), rims[1, z]], 0)
        sums = []
        for s in range(4):
            matrix = along_matrix(along[pl.ds(s * LAYERS + z, 1), :])
            y = along_sum(x[GROUP * s : GROUP * (s + 1)], matrix)
            sums.append(doses[s, z] * y)
        fields[0, z] = silicon * sums[1]
        fields[1, z] = silicon * sums[2]
        fields[2, z] = pair
        fixed[0, z] = silicon * sums[0]
        fixed[1, z] = silicon * (before + sums[3])
    for z in range(LAYERS):
        silicon = (fields[2, z] > 0.0).astype(F32)
        belows = [fields[f, z - 1] for f in range(3)] if z > 0 else NONE
        aboves = [fields[f, z + 1] for f in range(3)] if z < LAYERS - 1 else NONE
        centers = [fields[f, z] for f in range(3)]
        mobile, others = substep(spreads, rates, silicon, centers, belows, aboves, fixed[0, z], fixed[1, z], GROUP)
        for f in range(3):
            late[f, z] = mobile[f]
            if z in (0, 3):
                outer[f, z // 3] = fields[f, z, :ROWS]
        for f in range(2):
            still[f, z] = others[f][:ROWS]


def react_kernel(step, spreads, rates, outer, late, still, pairs, rims_own, payload, *refs):
    result, near_late, own_late, done, sems = refs[-5:]
    odd = lax.rem(lax.axis_index("depth"), 2)
    side = odd if step == 0 else 1 - odd

    def inward(i):
        return i + side * (3 - 2 * i)

    def pairs_of(z):
        return pairs[pl.ds(pl.multiple_of(ROWS * z, ROWS), ROWS), :].astype(F32)

    def sent(i):
        return payload[pl.ds(16 * i, 16), :].astype(F32)

    def known(i):
        return sent(7 + i)

    packed, lines = sent(4)[:8], sent(4)[8:]

    def implanted(i, x):
        line = lines[i : i + 1]
        dose = line[:, 128:129] + line[:, 256:257] + line[:, 384:385]
        return dose * along_sum(x, along_matrix(line[:, :128]))

    pair = jnp.concatenate([known(0), unpacked_rim(packed, 2)], 0)
    silicon = (pair > 0.0).astype(F32)
    near = [
        silicon * implanted(0, jnp.concatenate([sent(0), unpacked_rim(packed, 0)], 0)),
        silicon * implanted(1, jnp.concatenate([sent(1), unpacked_rim(packed, 1)], 0)),
        pair,
    ]
    silicon = silicon[:ROWS]
    arsenic = silicon * implanted(2, sent(2))
    clusters = silicon * (known(1) + implanted(3, sent(3)))
    far_pair = known(2)
    far_silicon = (far_pair > 0.0).astype(F32)
    far = [far_silicon * implanted(4, sent(5)), far_silicon * implanted(5, sent(6)), far_pair]
    beside = [outer[f, side] for f in range(3)]
    z = inward(0)
    own_pair = jnp.concatenate([pairs_of(z), rims_own[0, z]], 0)
    own_silicon = (own_pair > 0.0).astype(F32)
    for f in range(3):
        own_late[f] = late[f, z] + own_silicon * (spreads[f] * near[f])

    def copy(f, i):
        return pltpu.make_async_copy(done.at[f, i], result.at[f, inward(i)], sems.at[f, i])

    for i in (1, 0):
        at, beyond = inward(i), inward(i + 1)
        if i == 0:
            mobile, _ = substep(spreads, rates, silicon, near, far, beside, arsenic, clusters, ROWS)
            for f in range(3):
                near_late[f] = mobile[f]
        own_silicon = (pairs_of(at) > 0.0).astype(F32)
        centers = [late[f, at] if i else own_late[f] for f in range(3)]
        outers = [own_late[f] if i else near_late[f] for f in range(3)]
        inners = [late[f, beyond] for f in range(3)]
        mobile, others = substep(
            spreads, rates, own_silicon, centers, outers, inners, still[0, at], still[1, at], ROWS
        )
        for f, new in enumerate((others[0], *mobile, others[1])):
            done[f, i] = new
            copy(f, i).start()
    for i in (1, 0):
        for f in range(5):
            copy(f, i).wait()


def moved(array, axis, size, source):
    route = [(source(i), i) for i in range(size) if source(i) is not None and 0 <= source(i) < size]
    return lax.ppermute(array, axis, route)


def lanes(core0, core1):
    return lambda i: i + core0 if i % 2 == 0 else (None if core1 is None else i + core1)


def body(
    fin_mask,
    stopping_power,
    pairs_before,
    clusters_before,
    taps_across,
    taps_along,
    tilt_shift,
    layer_doses,
    diffusivity,
    reaction_rates,
):
    couples = [[2 * i, 2 * i + 1] for i in range(LATS // 2)]

    def shared(array):
        return lax.all_gather(array, "lat", axis_index_groups=couples)

    core = lax.rem(lax.axis_index("lat"), 2)
    silicon = fin_mask.astype(BF16)
    source = silicon * stopping_power
    pair = silicon * pairs_before
    source, pair = lax.optimization_barrier((source.reshape(64, LENGTH), pair))
    mine = shared(source).reshape(128, LENGTH)
    far = moved(mine, "lat", LATS, lanes(-4, 4))
    clusters, _ = lax.optimization_barrier((clusters_before, mine))
    first = [pair[:, :2], clusters[:, :1], clusters[:, :1]]
    last = [clusters[:, 15:], clusters[:, 15:], pair[:, 14:]]
    first, last = (jnp.concatenate(rows, 1).reshape(16, LENGTH) for rows in (first, last))
    outward, inward = jnp.where(core == 0, first, last), jnp.where(core == 0, last, first)
    pair = pair.reshape(64, LENGTH)
    received = moved(jnp.concatenate([mine, outward], 0), "lat", LATS, lanes(-1, 1))
    corner = jnp.pad(source.reshape(LAYERS, ROWS, LENGTH)[:, :2], ((0, 0), (0, 2), (0, 0))).reshape(16, LENGTH)
    corner = moved(corner, "lat", LATS, lambda i: None if i % 2 == 0 else i + 5)
    across_bands, early_down, early_up = call(
        prepare_kernel,
        (shape((LAYERS, 4 * GROUP, 256), F32), shape((64, LENGTH), BF16), shape((64, LENGTH), BF16)),
        (tilt_shift, layer_doses, taps_across, taps_along, pair, clusters_before),
        scalars=2,
        scratch=[pltpu.VMEM((16, 128), F32), pltpu.VMEM((16, 128), F32), pltpu.VMEM((32, LENGTH), F32)],
    )
    near = shared(jnp.concatenate([received[:128], inward], 0))
    far, near, early_down, early_up = lax.optimization_barrier((far, near, early_down, early_up))
    far = shared(far)
    spread, to_even, to_odd, rims = call(
        across_kernel,
        (
            shape((LAYERS, 4 * GROUP, LENGTH), BF16),
            shape((160, LENGTH), BF16),
            shape((160, LENGTH), BF16),
            shape((2, LAYERS, 8, LENGTH), F32),
        ),
        (mine.reshape(2, 64, LENGTH), near, received, far, corner, across_bands, early_down, early_up),
        scratch=[pltpu.VMEM((LAYERS, WINDOW, LENGTH), BF16)],
    )
    from_odd = moved(to_odd, "depth", DEPTHS, lanes(-1, 1))
    from_even = moved(to_even, "depth", DEPTHS, lanes(1, -1))
    outer, late, still = call(
        along_kernel,
        (
            shape((3, 2, ROWS, LENGTH), F32),
            shape((3, LAYERS, GROUP, LENGTH), F32),
            shape((2, LAYERS, ROWS, LENGTH), F32),
        ),
        (diffusivity, reaction_rates, layer_doses, spread, taps_along, pair, clusters_before, rims),
        scalars=3,
        scratch=[
            pltpu.VMEM((3, LAYERS, GROUP, LENGTH), F32),
            pltpu.VMEM((2, LAYERS, GROUP, LENGTH), F32),
            pltpu.VMEM((16, 128), F32),
        ],
    )
    scratch = [
        pltpu.VMEM((3, ROWS, LENGTH), F32),
        pltpu.VMEM((3, GROUP, LENGTH), F32),
        pltpu.VMEM((5, 2, ROWS, LENGTH), F32),
        pltpu.SemaphoreType.DMA((5, 2)),
    ]
    given = (diffusivity, reaction_rates, outer, late, still, pair, rims)
    for step, payload in enumerate((from_odd, from_even)):
        args = (*given, payload) if step == 0 else (*given, payload, result)
        result = call(
            functools.partial(react_kernel, step),
            shape((5, LAYERS, ROWS, LENGTH), F32),
            args,
            scalars=2,
            hbm=(8,),
            hbm_out=True,
            scratch=scratch,
            aliases={8: 0} if step else {},
        )
    return result


def solution(mesh):
    return jax.shard_map(
        body,
        mesh=mesh,
        in_specs=(
            P("depth", "lat", None),
            P("depth", "lat", None),
            P("depth", "lat", None),
            P("depth", "lat", None),
            P(None, "depth", None),
            P(None, "depth", None),
            P("depth"),
            P(None, "depth"),
            P(),
            P(),
        ),
        out_specs=P(None, "depth", "lat", None),
        check_vma=False,
    )
```

```python
import functools

import jax
import jax.numpy as jnp
from jax import lax
from jax.experimental import pallas as pl
from jax.experimental.pallas import tpu as pltpu
from jax.sharding import PartitionSpec as P

TAPS = 97
HALF = 48
LAYERS = 4
ROWS = 16
LENGTH = 1024
GROUP = 24
WINDOW = 176
LATS = 64
DEPTHS = 8
F32 = jnp.float32
BF16 = jnp.bfloat16
MEMORY = 32 * 1024 * 1024


def call(kernel, outs, args, scalars=0, hbm=(), hbm_out=False, scratch=(), flops=1000000, size=2000000):
    def space(i):
        return pltpu.SMEM if i < scalars else pltpu.HBM if i in hbm else pltpu.VMEM

    out_space = pltpu.HBM if hbm_out else pltpu.VMEM
    return pl.pallas_call(
        kernel,
        out_shape=outs,
        in_specs=[pl.BlockSpec(memory_space=space(i)) for i in range(len(args))],
        out_specs=jax.tree.map(lambda _: pl.BlockSpec(memory_space=out_space), outs),
        scratch_shapes=list(scratch),
        compiler_params=pltpu.CompilerParams(vmem_limit_bytes=MEMORY),
        cost_estimate=pl.CostEstimate(flops=flops, bytes_accessed=size, transcendentals=0),
    )(*args)


def shape(dims, dtype):
    return jax.ShapeDtypeStruct(dims, dtype)


def tile(z):
    return pl.ds(ROWS * z, ROWS)


def along_matrix(line):
    wide = jnp.concatenate([line, jnp.zeros_like(line)], 1)
    wide = jnp.broadcast_to(wide, (128, 256))
    return pltpu.roll(wide, 16, 1, stride=1, stride_axis=0).astype(BF16)


def own_core():
    return lax.rem(lax.axis_index("lat"), 2)


def wide_taps(taps, lines):
    lines[...] = jnp.zeros_like(lines)
    for s in range(4):
        lines[pl.ds(s * LAYERS, LAYERS), :TAPS] = taps[s].astype(F32)


def pair_edges(following, previous):
    sub = lax.broadcasted_iota(jnp.int32, (8, LENGTH), 0)
    return jnp.where(sub < 2, following, jnp.where(sub >= 6, previous, 0.0))


def cluster_edges(following, previous):
    sub = lax.broadcasted_iota(jnp.int32, (8, LENGTH), 0)
    following = pltpu.roll(following, 6, 0)
    previous = pltpu.roll(previous, 2, 0)
    return jnp.where(sub == 0, following, jnp.where(sub == 7, previous, 0.0))


SENT = ((1, 0), (2, 0), (0, 0), (3, 0), (1, 1), (2, 1))


def prepare_kernel(tilt, doses, taps_across, taps_along, pair, clusters, across_bands, down, up, early_even, across, taps, lines):
    wide_taps(taps_across, across)
    lane = lax.broadcasted_iota(jnp.int32, (GROUP, 256), 1)
    group = lax.broadcasted_iota(jnp.int32, (8, 256), 0)
    for z in range(LAYERS):
        offset = ROWS - 8 + ROWS * own_core() + tilt[z]
        for s in range(4):
            line = across[pl.ds(s * LAYERS + z, 1), :]
            wide = jnp.concatenate([line, jnp.zeros_like(line)], 1)
            wide = pltpu.roll(jnp.broadcast_to(wide, (8, 256)), offset, 1)
            band = pltpu.roll(jnp.broadcast_to(wide[:1], (32, 256)), 0, 1, stride=1, stride_axis=0)
            last = jnp.where(group < 2, band[24:], band[:8])
            band = jnp.concatenate([band[8:24], last], 0)
            tail = pltpu.roll(band, 4 * z, 1) if z else band
            tail = jnp.where((lane >= 160 + 4 * z) & (lane < 162 + 4 * z), tail, 0.0)
            across_bands[z, pl.ds(s * GROUP, GROUP), :] = jnp.where(lane < 160, band, tail)
    wide_taps(taps_along, taps)
    lines[...] = jnp.zeros_like(lines)
    for side, (out, near, far) in enumerate(((down, 0, 1), (up, 3, 2))):
        for i, (s, distance) in enumerate(SENT):
            z = far if distance else near
            row = pl.ds(16 * side + 8 + i, 1)
            lines[row, pl.ds(0, 128)] = taps[pl.ds(s * LAYERS + z, 1), :]
            dose = jnp.full((1, 128), doses[s, z], F32)
            for part in range(1, 4):
                rounded = dose.astype(BF16).astype(F32)
                lines[row, pl.ds(128 * part, 128)] = rounded
                dose = dose - rounded
        out[pl.ds(0, 16), :] = pair[tile(near), :]
        out[pl.ds(16, 16), :] = clusters[near]
        out[pl.ds(32, 16), :] = pair[tile(far), :]
        out[pl.ds(48, 16), :] = lines[pl.ds(16 * side, 16), :].astype(BF16)
    odd = lax.rem(lax.axis_index("depth"), 2)

    @pl.when(odd == 0)
    def _():
        early_even[...] = up[pl.ds(0, 48), :]

    @pl.when(odd == 1)
    def _():
        early_even[...] = down[pl.ds(0, 48), :]


def packed_rims(fields):
    sub = lax.broadcasted_iota(jnp.int32, (8, LENGTH), 0)
    total = jnp.where((sub == 0) | (sub == 7), fields[0], 0.0)
    for i, field in enumerate(fields[1:], 1):
        total = jnp.where(sub == i, pltpu.roll(field, i, 0), total)
        total = jnp.where(sub == 7 - i, pltpu.roll(field, 8 - i, 0), total)
    return total


def unpacked_rim(packed, i):
    sub = lax.broadcasted_iota(jnp.int32, (8, LENGTH), 0)
    following = pltpu.roll(packed, 8 - i, 0) if i else packed
    previous = pltpu.roll(packed, i, 0) if i else packed
    return jnp.where(sub == 0, following, jnp.where(sub == 7, previous, 0.0))


def across_kernel(
    mine, near, received, far, corner, bands, early_down, early_up, spread, across_even, across_odd, rims, window
):
    core = own_core()
    payloads = ({}, {})
    for payload, early in zip(payloads, (early_down, early_up)):
        payload[112, 48] = early[pl.ds(0, 48), :]
    for z in range(LAYERS):
        at, also = tile(z), pl.ds(64 + ROWS * z, ROWS)
        parts = [far[0, at, :], far[0, also, :], near[0, at, :], near[0, also, :]]
        parts += [mine[0, at, :], mine[1, at, :], near[1, at, :], near[1, also, :]]
        parts += [far[1, at, :], far[1, also, :], corner[...]]
        for i, part in enumerate(parts):
            window[z, pl.ds(16 * i, 16), :] = part
        x = jnp.dot(bands[z].astype(BF16)[:, :WINDOW], window[z], preferred_element_type=F32)
        spread[z] = x.astype(BF16)
        half = slice(8 * (z // 2), 8 * (z // 2) + 8)
        at = pl.ds(128, 16)
        other = received[at, :].astype(F32)
        following = jnp.where(core == 0, near[1, at, :].astype(F32), other)[half]
        previous = jnp.where(core == 0, other, near[0, at, :].astype(F32))[half]
        if z % 2:
            following = pltpu.roll(following, 4, 0)
        else:
            previous = pltpu.roll(previous, 4, 0)
        rims[0, z] = pair_edges(following, previous)
        rims[1, z] = cluster_edges(following, previous)
        payload = payloads[z // 2]
        own = [x[GROUP * s : GROUP * s + ROWS].astype(BF16) for s in range(4)]
        rim = [x[GROUP * s + ROWS : GROUP * s + GROUP] for s in range(4)]
        if z in (0, 3):
            for i, s in enumerate((1, 2, 0, 3)):
                payload[16 * i, 16] = own[s]
            lines = (early_down if z < 2 else early_up)[pl.ds(48, 16), :].astype(F32)[8:]
            packed = packed_rims((rim[1], rim[2], rims[0, z]))
            payload[64, 16] = jnp.concatenate([packed, lines], 0).astype(BF16)
        else:
            payload[80, 16] = own[1]
            payload[96, 16] = own[2]

    def write(payload, out):
        for (start, size), value in payload.items():
            if start < out.shape[0]:
                out[pl.ds(start, size), :] = value

    odd = lax.rem(lax.axis_index("depth"), 2)

    @pl.when(odd == 0)
    def _():
        write(payloads[0], across_odd)
        write(payloads[1], across_even)

    @pl.when(odd == 1)
    def _():
        write(payloads[0], across_even)
        write(payloads[1], across_odd)


def along_sum(x, matrix):
    rows = x.shape[0]
    zeros = jnp.zeros((rows, 64), F32)
    wide = jnp.concatenate([zeros, x, zeros], 1)
    blocks = LENGTH // 128
    stacked = jnp.concatenate([wide[:, 128 * b : 128 * b + 256] for b in range(blocks)], 0).astype(BF16)
    y = lax.dot_general(stacked, matrix, (((1,), (1,)), ((), ())), preferred_element_type=F32)
    return jnp.concatenate([y[rows * b : rows * (b + 1)] for b in range(blocks)], 1)


def laplace(center, below, above, rows):
    total = center.shape[0]
    inner = center[:rows]
    lane = lax.broadcasted_iota(jnp.int32, (rows, 128), 1)
    right = pltpu.roll(inner, LENGTH - 1, 1)
    left = pltpu.roll(inner, 1, 1)
    right = jnp.concatenate([right[:, :-128], jnp.where(lane == 127, 0.0, right[:, -128:])], 1)
    left = jnp.concatenate([jnp.where(lane == 0, 0.0, left[:, :128]), left[:, 128:]], 1)
    near = right + left
    near = near + pltpu.roll(center, total - 1, 0)[:rows] + pltpu.roll(center, 1, 0)[:rows]
    for layer in (below, above):
        if layer is not None:
            near = near + layer[:rows]
    return near - 6.0 * inner


def substep(spreads, rates, silicon, centers, belows, aboves, arsenic, clusters, rows):
    inter, vacancy, pair = (c[:rows] for c in centers)
    flows = [
        silicon * (spreads[f] * laplace(centers[f], belows[f], aboves[f], rows)) for f in range(3)
    ]
    recombine = rates[0] * inter * vacancy
    pairing = rates[1] * arsenic * inter - rates[2] * pair
    clustering = rates[3] * inter * inter - rates[4] * clusters
    new_inter = inter + (flows[0] - recombine - pairing - 2.0 * clustering)
    new_vacancy = vacancy + (flows[1] - recombine)
    new_pair = pair + (flows[2] + pairing)
    return (new_inter, new_vacancy, new_pair), (arsenic - pairing, clusters + clustering)


NONE = (None, None, None)


def along_kernel(spreads, rates, doses, spread, taps_along, pairs, clusters, rims, outer, late, still, inner, fields, fixed, along):
    wide_taps(taps_along, along)
    for z in range(LAYERS):
        x = spread[z].astype(F32)
        pair = jnp.concatenate([pairs[tile(z), :].astype(F32), rims[0, z]], 0)
        silicon = (pair > 0.0).astype(F32)
        before = jnp.concatenate([clusters[z].astype(F32), rims[1, z]], 0)
        sums = []
        for s in range(4):
            matrix = along_matrix(along[pl.ds(s * LAYERS + z, 1), :])
            y = along_sum(x[GROUP * s : GROUP * (s + 1)], matrix)
            sums.append(doses[s, z] * y)
        fields[0, z] = silicon * sums[1]
        fields[1, z] = silicon * sums[2]
        fields[2, z] = pair
        fixed[0, z] = silicon * sums[0]
        fixed[1, z] = silicon * (before + sums[3])
    for z in range(LAYERS):
        silicon = (fields[2, z] > 0.0).astype(F32)
        belows = [fields[f, z - 1] for f in range(3)] if z > 0 else NONE
        aboves = [fields[f, z + 1] for f in range(3)] if z < LAYERS - 1 else NONE
        centers = [fields[f, z] for f in range(3)]
        mobile, others = substep(spreads, rates, silicon, centers, belows, aboves, fixed[0, z], fixed[1, z], GROUP)
        for f in range(3):
            late[f, z] = mobile[f]
            if z in (0, 3):
                outer[f, z // 3] = fields[f, z, :ROWS]
        for f in range(2):
            still[f, z] = others[f][:ROWS]
    for z in (1, 2):
        silicon = (pairs[tile(z), :].astype(F32) > 0.0).astype(F32)
        centers, belows, aboves = ([late[f, at] for f in range(3)] for at in (z, z - 1, z + 1))
        mobile, others = substep(spreads, rates, silicon, centers, belows, aboves, still[0, z], still[1, z], ROWS)
        for f, new in enumerate((others[0], *mobile, others[1])):
            inner[f, z - 1] = new


def react_kernel(step, spreads, rates, outer, late, still, inner, pairs, rims_own, payload, *refs):
    if step == 0:
        done, near_late, own_late = refs
    else:
        early, earlier, result, near_late, own_late, done, sems = refs
    odd = lax.rem(lax.axis_index("depth"), 2)
    side = odd if step == 0 else 1 - odd

    def inward(i):
        return i + side * (3 - 2 * i)

    def copy(half, f, i):
        at = inward(i) if half else 3 - inward(i)
        return pltpu.make_async_copy((earlier, done)[half].at[f, i], result.at[f, at], sems.at[half, f, i])

    if step == 1:
        for i in range(2):
            for f in range(5):
                copy(0, f, i).start()

    def pairs_of(z):
        return pairs[pl.ds(pl.multiple_of(ROWS * z, ROWS), ROWS), :].astype(F32)

    def sent(i):
        return payload[pl.ds(16 * i, 16), :].astype(F32)

    def known(i):
        return early[pl.ds(16 * i, 16), :].astype(F32) if step else sent(7 + i)

    packed, lines = sent(4)[:8], sent(4)[8:]

    def implanted(i, x):
        line = lines[i : i + 1]
        dose = line[:, 128:129] + line[:, 256:257] + line[:, 384:385]
        return dose * along_sum(x, along_matrix(line[:, :128]))

    pair = jnp.concatenate([known(0), unpacked_rim(packed, 2)], 0)
    silicon = (pair > 0.0).astype(F32)
    near = [
        silicon * implanted(0, jnp.concatenate([sent(0), unpacked_rim(packed, 0)], 0)),
        silicon * implanted(1, jnp.concatenate([sent(1), unpacked_rim(packed, 1)], 0)),
        pair,
    ]
    silicon = silicon[:ROWS]
    arsenic = silicon * implanted(2, sent(2))
    clusters = silicon * (known(1) + implanted(3, sent(3)))
    far_pair = known(2)
    far_silicon = (far_pair > 0.0).astype(F32)
    far = [far_silicon * implanted(4, sent(5)), far_silicon * implanted(5, sent(6)), far_pair]
    beside = [outer[f, side] for f in range(3)]
    z = inward(0)
    own_pair = jnp.concatenate([pairs_of(z), rims_own[0, z]], 0)
    own_silicon = (own_pair > 0.0).astype(F32)
    inner_silicon = (pairs_of(inward(1)) > 0.0).astype(F32)
    for f in range(3):
        change = own_silicon * (spreads[f] * near[f])
        own_late[f] = late[f, z] + change
        done[f + 1, 1] = inner[f + 1, side] + inner_silicon * (spreads[f] * change[:ROWS])
    for f in (0, 4):
        done[f, 1] = inner[f, side]
    if step == 1:
        for f in range(5):
            copy(1, f, 1).start()
    mobile, _ = substep(spreads, rates, silicon, near, far, beside, arsenic, clusters, ROWS)
    for f in range(3):
        near_late[f] = mobile[f]
    centers = [own_late[f] for f in range(3)]
    outers = [near_late[f] for f in range(3)]
    inners = [late[f, inward(1)] for f in range(3)]
    mobile, others = substep(
        spreads, rates, own_silicon[:ROWS], centers, outers, inners, still[0, z], still[1, z], ROWS
    )
    for f, new in enumerate((others[0], *mobile, others[1])):
        done[f, 0] = new
        if step == 1:
            copy(1, f, 0).start()
    if step == 1:
        for half in range(2):
            for i in range(2):
                for f in range(5):
                    copy(half, f, i).wait()


def moved(array, axis, size, source):
    route = [(source(i), i) for i in range(size) if source(i) is not None and 0 <= source(i) < size]
    return lax.ppermute(array, axis, route)


def lanes(core0, core1):
    return lambda i: i + core0 if i % 2 == 0 else (None if core1 is None else i + core1)


def body(
    fin_mask,
    stopping_power,
    pairs_before,
    clusters_before,
    taps_across,
    taps_along,
    tilt_shift,
    layer_doses,
    diffusivity,
    reaction_rates,
):
    couples = [[2 * i, 2 * i + 1] for i in range(LATS // 2)]

    def shared(array):
        return lax.all_gather(array, "lat", axis_index_groups=couples)

    core = lax.rem(lax.axis_index("lat"), 2)
    silicon = fin_mask.astype(BF16)
    source = silicon * stopping_power
    pair = silicon * pairs_before
    clusters = silicon * clusters_before
    source, pair, clusters = lax.optimization_barrier((source.reshape(64, LENGTH), pair, clusters))
    mine = shared(source).reshape(128, LENGTH)
    far = moved(mine, "lat", LATS, lanes(-4, 4))
    first = [pair[:, :2], clusters[:, :1], clusters[:, :1]]
    last = [clusters[:, 15:], clusters[:, 15:], pair[:, 14:]]
    first, last = (jnp.concatenate(rows, 1).reshape(16, LENGTH) for rows in (first, last))
    outward, inward = jnp.where(core == 0, first, last), jnp.where(core == 0, last, first)
    pair = pair.reshape(64, LENGTH)
    received = moved(jnp.concatenate([mine, outward], 0), "lat", LATS, lanes(-1, 1))
    corner = jnp.pad(source.reshape(LAYERS, ROWS, LENGTH)[:, :2], ((0, 0), (0, 2), (0, 0))).reshape(16, LENGTH)
    corner = moved(corner, "lat", LATS, lambda i: None if i % 2 == 0 else i + 5)
    across_bands, early_down, early_up, early_even = call(
        prepare_kernel,
        (
            shape((LAYERS, 4 * GROUP, 256), F32),
            shape((64, LENGTH), BF16),
            shape((64, LENGTH), BF16),
            shape((48, LENGTH), BF16),
        ),
        (tilt_shift, layer_doses, taps_across, taps_along, pair, clusters),
        scalars=2,
        scratch=[pltpu.VMEM((16, 128), F32), pltpu.VMEM((16, 128), F32), pltpu.VMEM((32, LENGTH), F32)],
    )
    early_even = moved(early_even, "depth", DEPTHS, lanes(1, -1))
    near = shared(jnp.concatenate([received[:128], inward], 0))
    far, near, early_down, early_up = lax.optimization_barrier((far, near, early_down, early_up))
    far = shared(far)
    spread, to_even, to_odd, rims = call(
        across_kernel,
        (
            shape((LAYERS, 4 * GROUP, LENGTH), BF16),
            shape((112, LENGTH), BF16),
            shape((160, LENGTH), BF16),
            shape((2, LAYERS, 8, LENGTH), F32),
        ),
        (mine.reshape(2, 64, LENGTH), near, received, far, corner, across_bands, early_down, early_up),
        scratch=[pltpu.VMEM((LAYERS, WINDOW, LENGTH), BF16)],
    )
    to_even, to_odd, early_even = lax.optimization_barrier((to_even, to_odd, early_even))
    from_odd = moved(to_odd, "depth", DEPTHS, lanes(-1, 1))
    from_even = moved(to_even, "depth", DEPTHS, lanes(1, -1))
    outer, late, still, inner = call(
        along_kernel,
        (
            shape((3, 2, ROWS, LENGTH), F32),
            shape((3, LAYERS, GROUP, LENGTH), F32),
            shape((2, LAYERS, ROWS, LENGTH), F32),
            shape((5, 2, ROWS, LENGTH), F32),
        ),
        (diffusivity, reaction_rates, layer_doses, spread, taps_along, pair, clusters, rims),
        scalars=3,
        scratch=[
            pltpu.VMEM((3, LAYERS, GROUP, LENGTH), F32),
            pltpu.VMEM((2, LAYERS, GROUP, LENGTH), F32),
            pltpu.VMEM((16, 128), F32),
        ],
    )
    given = (diffusivity, reaction_rates, outer, late, still, inner, pair, rims)
    scratch = [pltpu.VMEM((3, ROWS, LENGTH), F32), pltpu.VMEM((3, GROUP, LENGTH), F32)]
    half = shape((5, 2, ROWS, LENGTH), F32)
    earlier = call(
        functools.partial(react_kernel, 0),
        half,
        (*given, from_odd),
        scalars=2,
        scratch=scratch,
    )
    return call(
        functools.partial(react_kernel, 1),
        shape((5, LAYERS, ROWS, LENGTH), F32),
        (*given, from_even, early_even, earlier),
        scalars=2,
        hbm_out=True,
        scratch=[*scratch, pltpu.VMEM(half.shape, F32), pltpu.SemaphoreType.DMA((2, 5, 2))],
    )


def solution(mesh):
    return jax.shard_map(
        body,
        mesh=mesh,
        in_specs=(
            P("depth", "lat", None),
            P("depth", "lat", None),
            P("depth", "lat", None),
            P("depth", "lat", None),
            P(None, "depth", None),
            P(None, "depth", None),
            P("depth"),
            P(None, "depth"),
            P(),
            P(),
        ),
        out_specs=P(None, "depth", "lat", None),
        check_vma=False,
    )
```

```python
import jax
import jax.numpy as jnp
from jax import lax
from jax.experimental import pallas as pl
from jax.experimental.pallas import tpu as pltpu
from jax.sharding import PartitionSpec as P

TAPS = 97
HALF = 48
LAYERS = 4
ROWS = 16
LENGTH = 1024
GROUP = 24
WINDOW = 176
LATS = 64
DEPTHS = 8
F32 = jnp.float32
BF16 = jnp.bfloat16
MEMORY = 32 * 1024 * 1024


def call(kernel, outs, args, scalars=0, hbm=(), hbm_out=False, scratch=(), flops=1000000, size=2000000):
    def space(i):
        return pltpu.SMEM if i < scalars else pltpu.HBM if i in hbm else pltpu.VMEM

    out_space = pltpu.HBM if hbm_out else pltpu.VMEM
    return pl.pallas_call(
        kernel,
        out_shape=outs,
        in_specs=[pl.BlockSpec(memory_space=space(i)) for i in range(len(args))],
        out_specs=jax.tree.map(lambda _: pl.BlockSpec(memory_space=out_space), outs),
        scratch_shapes=list(scratch),
        compiler_params=pltpu.CompilerParams(vmem_limit_bytes=MEMORY),
        cost_estimate=pl.CostEstimate(flops=flops, bytes_accessed=size, transcendentals=0),
    )(*args)


def shape(dims, dtype):
    return jax.ShapeDtypeStruct(dims, dtype)


def tile(z):
    return pl.ds(ROWS * z, ROWS)


def along_matrix(line):
    wide = jnp.concatenate([line, jnp.zeros_like(line)], 1)
    wide = jnp.broadcast_to(wide, (128, 256))
    return pltpu.roll(wide, 16, 1, stride=1, stride_axis=0).astype(BF16)


def own_core():
    return lax.rem(lax.axis_index("lat"), 2)


def wide_taps(taps, lines):
    lines[...] = jnp.zeros_like(lines)
    for s in range(4):
        lines[pl.ds(s * LAYERS, LAYERS), :TAPS] = taps[s].astype(F32)


def pair_edges(following, previous):
    sub = lax.broadcasted_iota(jnp.int32, (8, LENGTH), 0)
    return jnp.where(sub < 2, following, jnp.where(sub >= 6, previous, 0.0))


def cluster_edges(following, previous):
    sub = lax.broadcasted_iota(jnp.int32, (8, LENGTH), 0)
    following = pltpu.roll(following, 6, 0)
    previous = pltpu.roll(previous, 2, 0)
    return jnp.where(sub == 0, following, jnp.where(sub == 7, previous, 0.0))


SENT = ((1, 0), (2, 0), (0, 0), (3, 0), (1, 1), (2, 1))


def prepare_kernel(tilt, doses, taps_across, taps_along, pair, clusters, across_bands, down, up, early_even, across, taps, lines):
    wide_taps(taps_across, across)
    lane = lax.broadcasted_iota(jnp.int32, (GROUP, 256), 1)
    group = lax.broadcasted_iota(jnp.int32, (8, 256), 0)
    for z in range(LAYERS):
        offset = ROWS - 8 + ROWS * own_core() + tilt[z]
        for s in range(4):
            line = across[pl.ds(s * LAYERS + z, 1), :]
            wide = jnp.concatenate([line, jnp.zeros_like(line)], 1)
            wide = pltpu.roll(jnp.broadcast_to(wide, (8, 256)), offset, 1)
            band = pltpu.roll(jnp.broadcast_to(wide[:1], (32, 256)), 0, 1, stride=1, stride_axis=0)
            last = jnp.where(group < 2, band[24:], band[:8])
            band = jnp.concatenate([band[8:24], last], 0)
            tail = pltpu.roll(band, 4 * z, 1) if z else band
            tail = jnp.where((lane >= 160 + 4 * z) & (lane < 162 + 4 * z), tail, 0.0)
            across_bands[z, pl.ds(s * GROUP, GROUP), :] = jnp.where(lane < 160, band, tail)
    wide_taps(taps_along, taps)
    lines[...] = jnp.zeros_like(lines)
    for side, (out, near, far) in enumerate(((down, 0, 1), (up, 3, 2))):
        for i, (s, distance) in enumerate(SENT):
            z = far if distance else near
            row = pl.ds(16 * side + 8 + i, 1)
            lines[row, pl.ds(0, 128)] = taps[pl.ds(s * LAYERS + z, 1), :]
            dose = jnp.full((1, 128), doses[s, z], F32)
            for part in range(1, 4):
                rounded = dose.astype(BF16).astype(F32)
                lines[row, pl.ds(128 * part, 128)] = rounded
                dose = dose - rounded
        out[pl.ds(0, 16), :] = pair[tile(near), :]
        out[pl.ds(16, 16), :] = clusters[near]
        out[pl.ds(32, 16), :] = pair[tile(far), :]
        out[pl.ds(48, 16), :] = lines[pl.ds(16 * side, 16), :].astype(BF16)
    odd = lax.rem(lax.axis_index("depth"), 2)

    @pl.when(odd == 0)
    def _():
        early_even[...] = up[pl.ds(0, 48), :]

    @pl.when(odd == 1)
    def _():
        early_even[...] = down[pl.ds(0, 48), :]


def packed_rims(fields):
    sub = lax.broadcasted_iota(jnp.int32, (8, LENGTH), 0)
    total = jnp.where((sub == 0) | (sub == 7), fields[0], 0.0)
    for i, field in enumerate(fields[1:], 1):
        total = jnp.where(sub == i, pltpu.roll(field, i, 0), total)
        total = jnp.where(sub == 7 - i, pltpu.roll(field, 8 - i, 0), total)
    return total


def unpacked_rim(packed, i):
    sub = lax.broadcasted_iota(jnp.int32, (8, LENGTH), 0)
    following = pltpu.roll(packed, 8 - i, 0) if i else packed
    previous = pltpu.roll(packed, i, 0) if i else packed
    return jnp.where(sub == 0, following, jnp.where(sub == 7, previous, 0.0))


def across_kernel(
    mine, near, received, far, corner, bands, early_down, early_up, spread, across_even, across_odd, rims, window
):
    core = own_core()
    payloads = ({}, {})
    for payload, early in zip(payloads, (early_down, early_up)):
        payload[112, 48] = early[pl.ds(0, 48), :]
    for z in range(LAYERS):
        at, also = tile(z), pl.ds(64 + ROWS * z, ROWS)
        parts = [far[0, at, :], far[0, also, :], near[0, at, :], near[0, also, :]]
        parts += [mine[0, at, :], mine[1, at, :], near[1, at, :], near[1, also, :]]
        parts += [far[1, at, :], far[1, also, :], corner[...]]
        for i, part in enumerate(parts):
            window[z, pl.ds(16 * i, 16), :] = part
        x = jnp.dot(bands[z].astype(BF16)[:, :WINDOW], window[z], preferred_element_type=F32)
        spread[z] = x.astype(BF16)
        half = slice(8 * (z // 2), 8 * (z // 2) + 8)
        at = pl.ds(128, 16)
        other = received[at, :].astype(F32)
        following = jnp.where(core == 0, near[1, at, :].astype(F32), other)[half]
        previous = jnp.where(core == 0, other, near[0, at, :].astype(F32))[half]
        if z % 2:
            following = pltpu.roll(following, 4, 0)
        else:
            previous = pltpu.roll(previous, 4, 0)
        rims[0, z] = pair_edges(following, previous)
        rims[1, z] = cluster_edges(following, previous)
        payload = payloads[z // 2]
        own = [x[GROUP * s : GROUP * s + ROWS].astype(BF16) for s in range(4)]
        rim = [x[GROUP * s + ROWS : GROUP * s + GROUP] for s in range(4)]
        if z in (0, 3):
            for i, s in enumerate((1, 2, 0, 3)):
                payload[16 * i, 16] = own[s]
            lines = (early_down if z < 2 else early_up)[pl.ds(48, 16), :].astype(F32)[8:]
            packed = packed_rims((rim[1], rim[2], rims[0, z]))
            payload[64, 16] = jnp.concatenate([packed, lines], 0).astype(BF16)
        else:
            payload[80, 16] = own[1]
            payload[96, 16] = own[2]

    def write(payload, out):
        for (start, size), value in payload.items():
            if start < out.shape[0]:
                out[pl.ds(start, size), :] = value

    odd = lax.rem(lax.axis_index("depth"), 2)

    @pl.when(odd == 0)
    def _():
        write(payloads[0], across_odd)
        write(payloads[1], across_even)

    @pl.when(odd == 1)
    def _():
        write(payloads[0], across_even)
        write(payloads[1], across_odd)


def along_sum(x, matrix):
    rows = x.shape[0]
    zeros = jnp.zeros((rows, 64), F32)
    wide = jnp.concatenate([zeros, x, zeros], 1)
    blocks = LENGTH // 128
    stacked = jnp.concatenate([wide[:, 128 * b : 128 * b + 256] for b in range(blocks)], 0).astype(BF16)
    y = lax.dot_general(stacked, matrix, (((1,), (1,)), ((), ())), preferred_element_type=F32)
    return jnp.concatenate([y[rows * b : rows * (b + 1)] for b in range(blocks)], 1)


def laplace(center, below, above, rows):
    total = center.shape[0]
    inner = center[:rows]
    lane = lax.broadcasted_iota(jnp.int32, (rows, 128), 1)
    right = pltpu.roll(inner, LENGTH - 1, 1)
    left = pltpu.roll(inner, 1, 1)
    right = jnp.concatenate([right[:, :-128], jnp.where(lane == 127, 0.0, right[:, -128:])], 1)
    left = jnp.concatenate([jnp.where(lane == 0, 0.0, left[:, :128]), left[:, 128:]], 1)
    near = right + left
    near = near + pltpu.roll(center, total - 1, 0)[:rows] + pltpu.roll(center, 1, 0)[:rows]
    for layer in (below, above):
        if layer is not None:
            near = near + layer[:rows]
    return near - 6.0 * inner


def substep(spreads, rates, silicon, centers, belows, aboves, arsenic, clusters, rows):
    inter, vacancy, pair = (c[:rows] for c in centers)
    flows = [
        silicon * (spreads[f] * laplace(centers[f], belows[f], aboves[f], rows)) for f in range(3)
    ]
    recombine = rates[0] * inter * vacancy
    pairing = rates[1] * arsenic * inter - rates[2] * pair
    clustering = rates[3] * inter * inter - rates[4] * clusters
    new_inter = inter + (flows[0] - recombine - pairing - 2.0 * clustering)
    new_vacancy = vacancy + (flows[1] - recombine)
    new_pair = pair + (flows[2] + pairing)
    return (new_inter, new_vacancy, new_pair), (arsenic - pairing, clusters + clustering)


NONE = (None, None, None)


def along_kernel(spreads, rates, doses, spread, taps_along, pairs, clusters, rims, outer, late, still, inner, fields, fixed, along):
    wide_taps(taps_along, along)
    for z in range(LAYERS):
        x = spread[z].astype(F32)
        pair = jnp.concatenate([pairs[tile(z), :].astype(F32), rims[0, z]], 0)
        silicon = (pair > 0.0).astype(F32)
        before = jnp.concatenate([clusters[z].astype(F32), rims[1, z]], 0)
        sums = []
        for s in range(4):
            matrix = along_matrix(along[pl.ds(s * LAYERS + z, 1), :])
            y = along_sum(x[GROUP * s : GROUP * (s + 1)], matrix)
            sums.append(doses[s, z] * y)
        fields[0, z] = silicon * sums[1]
        fields[1, z] = silicon * sums[2]
        fields[2, z] = pair
        fixed[0, z] = silicon * sums[0]
        fixed[1, z] = silicon * (before + sums[3])
    for z in range(LAYERS):
        silicon = (fields[2, z] > 0.0).astype(F32)
        belows = [fields[f, z - 1] for f in range(3)] if z > 0 else NONE
        aboves = [fields[f, z + 1] for f in range(3)] if z < LAYERS - 1 else NONE
        centers = [fields[f, z] for f in range(3)]
        mobile, others = substep(spreads, rates, silicon, centers, belows, aboves, fixed[0, z], fixed[1, z], GROUP)
        for f in range(3):
            late[f, z] = mobile[f]
            if z in (0, 3):
                outer[f, z // 3] = fields[f, z, :ROWS]
        for f in range(2):
            still[f, z] = others[f][:ROWS]
    for z in (1, 2):
        silicon = (pairs[tile(z), :].astype(F32) > 0.0).astype(F32)
        centers, belows, aboves = ([late[f, at] for f in range(3)] for at in (z, z - 1, z + 1))
        mobile, others = substep(spreads, rates, silicon, centers, belows, aboves, still[0, z], still[1, z], ROWS)
        for f, new in enumerate((others[0], *mobile, others[1])):
            inner[f, z - 1] = new


def react_kernel(step, spreads, rates, outer, late, still, inner, pairs, rims_own, payload, *refs):
    if step == 0:
        done, near_late, own_late = refs
    else:
        early, earlier, result, near_late, own_late, done, sems = refs
    odd = lax.rem(lax.axis_index("depth"), 2)
    side = odd if step == 0 else 1 - odd

    def inward(i):
        return i + side * (3 - 2 * i)

    def copy(half, f, i):
        at = inward(i) if half else 3 - inward(i)
        return pltpu.make_async_copy((earlier, done)[half].at[f, i], result.at[f, at], sems.at[half, f, i])

    if step == 1:
        for i in range(2):
            for f in range(5):
                copy(0, f, i).start()

    def pairs_of(z):
        return pairs[pl.ds(pl.multiple_of(ROWS * z, ROWS), ROWS), :].astype(F32)

    def sent(i):
        return payload[pl.ds(16 * i, 16), :].astype(F32)

    def known(i):
        return early[pl.ds(16 * i, 16), :].astype(F32) if step else sent(7 + i)

    packed, lines = sent(4)[:8], sent(4)[8:]

    def implanted(i, x):
        line = lines[i : i + 1]
        dose = line[:, 128:129] + line[:, 256:257] + line[:, 384:385]
        return dose * along_sum(x, along_matrix(line[:, :128]))

    pair = jnp.concatenate([known(0), unpacked_rim(packed, 2)], 0)
    silicon = (pair > 0.0).astype(F32)
    near = [
        silicon * implanted(0, jnp.concatenate([sent(0), unpacked_rim(packed, 0)], 0)),
        silicon * implanted(1, jnp.concatenate([sent(1), unpacked_rim(packed, 1)], 0)),
        pair,
    ]
    silicon = silicon[:ROWS]
    arsenic = silicon * implanted(2, sent(2))
    clusters = silicon * (known(1) + implanted(3, sent(3)))
    far_pair = known(2)
    far_silicon = (far_pair > 0.0).astype(F32)
    far = [far_silicon * implanted(4, sent(5)), far_silicon * implanted(5, sent(6)), far_pair]
    beside = [outer[f, side] for f in range(3)]
    z = inward(0)
    own_pair = jnp.concatenate([pairs_of(z), rims_own[0, z]], 0)
    own_silicon = (own_pair > 0.0).astype(F32)
    inner_silicon = (pairs_of(inward(1)) > 0.0).astype(F32)
    for f in range(3):
        change = own_silicon * (spreads[f] * near[f])
        own_late[f] = late[f, z] + change
        done[f + 1, 1] = inner[f + 1, side] + inner_silicon * (spreads[f] * change[:ROWS])
    for f in (0, 4):
        done[f, 1] = inner[f, side]
    if step == 1:
        for f in range(5):
            copy(1, f, 1).start()
    mobile, _ = substep(spreads, rates, silicon, near, far, beside, arsenic, clusters, ROWS)
    for f in range(3):
        near_late[f] = mobile[f]
    centers = [own_late[f] for f in range(3)]
    outers = [near_late[f] for f in range(3)]
    inners = [late[f, inward(1)] for f in range(3)]
    mobile, others = substep(
        spreads, rates, own_silicon[:ROWS], centers, outers, inners, still[0, z], still[1, z], ROWS
    )
    for f, new in enumerate((others[0], *mobile, others[1])):
        done[f, 0] = new
        if step == 1:
            copy(1, f, 0).start()
    if step == 1:
        for half in range(2):
            for i in range(2):
                for f in range(5):
                    copy(half, f, i).wait()


def both_kernel(*refs):
    given, (from_odd, from_even, early, result) = refs[:8], refs[8:12]
    near_odd, own_odd, near_even, own_even, earlier, done, sems = refs[12:]
    react_kernel(0, *given, from_odd, earlier, near_odd, own_odd)
    react_kernel(1, *given, from_even, early, earlier, result, near_even, own_even, done, sems)


def moved(array, axis, size, source):
    route = [(source(i), i) for i in range(size) if source(i) is not None and 0 <= source(i) < size]
    return lax.ppermute(array, axis, route)


def lanes(core0, core1):
    return lambda i: i + core0 if i % 2 == 0 else (None if core1 is None else i + core1)


def body(
    fin_mask,
    stopping_power,
    pairs_before,
    clusters_before,
    taps_across,
    taps_along,
    tilt_shift,
    layer_doses,
    diffusivity,
    reaction_rates,
):
    couples = [[2 * i, 2 * i + 1] for i in range(LATS // 2)]

    def shared(array):
        return lax.all_gather(array, "lat", axis_index_groups=couples)

    core = lax.rem(lax.axis_index("lat"), 2)
    silicon = fin_mask.astype(BF16)
    source = silicon * stopping_power
    pair = silicon * pairs_before
    clusters = silicon * clusters_before
    source, pair, clusters = lax.optimization_barrier((source.reshape(64, LENGTH), pair, clusters))
    mine = shared(source).reshape(128, LENGTH)
    far = moved(mine, "lat", LATS, lanes(-4, 4))
    first = [pair[:, :2], clusters[:, :1], clusters[:, :1]]
    last = [clusters[:, 15:], clusters[:, 15:], pair[:, 14:]]
    first, last = (jnp.concatenate(rows, 1).reshape(16, LENGTH) for rows in (first, last))
    outward, inward = jnp.where(core == 0, first, last), jnp.where(core == 0, last, first)
    pair = pair.reshape(64, LENGTH)
    received = moved(jnp.concatenate([mine, outward], 0), "lat", LATS, lanes(-1, 1))
    corner = jnp.pad(source.reshape(LAYERS, ROWS, LENGTH)[:, :2], ((0, 0), (0, 2), (0, 0))).reshape(16, LENGTH)
    corner = moved(corner, "lat", LATS, lambda i: None if i % 2 == 0 else i + 5)
    across_bands, early_down, early_up, early_even = call(
        prepare_kernel,
        (
            shape((LAYERS, 4 * GROUP, 256), F32),
            shape((64, LENGTH), BF16),
            shape((64, LENGTH), BF16),
            shape((48, LENGTH), BF16),
        ),
        (tilt_shift, layer_doses, taps_across, taps_along, pair, clusters),
        scalars=2,
        scratch=[pltpu.VMEM((16, 128), F32), pltpu.VMEM((16, 128), F32), pltpu.VMEM((32, LENGTH), F32)],
    )
    early_even = moved(early_even, "depth", DEPTHS, lanes(1, -1))
    near = shared(jnp.concatenate([received[:128], inward], 0))
    far, near, early_down, early_up = lax.optimization_barrier((far, near, early_down, early_up))
    far = shared(far)
    spread, to_even, to_odd, rims = call(
        across_kernel,
        (
            shape((LAYERS, 4 * GROUP, LENGTH), BF16),
            shape((112, LENGTH), BF16),
            shape((160, LENGTH), BF16),
            shape((2, LAYERS, 8, LENGTH), F32),
        ),
        (mine.reshape(2, 64, LENGTH), near, received, far, corner, across_bands, early_down, early_up),
        scratch=[pltpu.VMEM((LAYERS, WINDOW, LENGTH), BF16)],
    )
    to_even, to_odd, early_even = lax.optimization_barrier((to_even, to_odd, early_even))
    from_odd = moved(to_odd, "depth", DEPTHS, lanes(-1, 1))
    from_even = moved(to_even, "depth", DEPTHS, lanes(1, -1))
    outer, late, still, inner = call(
        along_kernel,
        (
            shape((3, 2, ROWS, LENGTH), F32),
            shape((3, LAYERS, GROUP, LENGTH), F32),
            shape((2, LAYERS, ROWS, LENGTH), F32),
            shape((5, 2, ROWS, LENGTH), F32),
        ),
        (diffusivity, reaction_rates, layer_doses, spread, taps_along, pair, clusters, rims),
        scalars=3,
        scratch=[
            pltpu.VMEM((3, LAYERS, GROUP, LENGTH), F32),
            pltpu.VMEM((2, LAYERS, GROUP, LENGTH), F32),
            pltpu.VMEM((16, 128), F32),
        ],
    )
    side_scratch = [pltpu.VMEM((3, ROWS, LENGTH), F32), pltpu.VMEM((3, GROUP, LENGTH), F32)]
    half = pltpu.VMEM((5, 2, ROWS, LENGTH), F32)
    return call(
        both_kernel,
        shape((5, LAYERS, ROWS, LENGTH), F32),
        (diffusivity, reaction_rates, outer, late, still, inner, pair, rims, from_odd, from_even, early_even),
        scalars=2,
        hbm_out=True,
        scratch=[*side_scratch, *side_scratch, half, half, pltpu.SemaphoreType.DMA((2, 5, 2))],
    )


def solution(mesh):
    return jax.shard_map(
        body,
        mesh=mesh,
        in_specs=(
            P("depth", "lat", None),
            P("depth", "lat", None),
            P("depth", "lat", None),
            P("depth", "lat", None),
            P(None, "depth", None),
            P(None, "depth", None),
            P("depth"),
            P(None, "depth"),
            P(),
            P(),
        ),
        out_specs=P(None, "depth", "lat", None),
        check_vma=False,
    )
```

```python
import jax
import jax.numpy as jnp
from jax import lax
from jax.experimental import pallas as pl
from jax.experimental.pallas import tpu as pltpu
from jax.sharding import PartitionSpec as P

TAPS = 97
HALF = 48
LAYERS = 4
ROWS = 16
LENGTH = 1024
GROUP = 24
WINDOW = 176
LATS = 64
DEPTHS = 8
F32 = jnp.float32
BF16 = jnp.bfloat16
MEMORY = 32 * 1024 * 1024


def call(kernel, outs, args, scalars=0, hbm=(), hbm_out=False, scratch=(), flops=1000000, size=2000000):
    def space(i):
        return pltpu.SMEM if i < scalars else pltpu.HBM if i in hbm else pltpu.VMEM

    out_space = pltpu.HBM if hbm_out else pltpu.VMEM
    return pl.pallas_call(
        kernel,
        out_shape=outs,
        in_specs=[pl.BlockSpec(memory_space=space(i)) for i in range(len(args))],
        out_specs=jax.tree.map(lambda _: pl.BlockSpec(memory_space=out_space), outs),
        scratch_shapes=list(scratch),
        compiler_params=pltpu.CompilerParams(vmem_limit_bytes=MEMORY),
        cost_estimate=pl.CostEstimate(flops=flops, bytes_accessed=size, transcendentals=0),
    )(*args)


def shape(dims, dtype):
    return jax.ShapeDtypeStruct(dims, dtype)


def tile(z):
    return pl.ds(ROWS * z, ROWS)


def along_matrix(line):
    wide = jnp.concatenate([line, jnp.zeros_like(line)], 1)
    wide = jnp.broadcast_to(wide, (128, 256))
    return pltpu.roll(wide, 16, 1, stride=1, stride_axis=0).astype(BF16)


def own_core():
    return lax.rem(lax.axis_index("lat"), 2)


def wide_taps(taps, lines):
    lines[...] = jnp.zeros_like(lines)
    for s in range(4):
        lines[pl.ds(s * LAYERS, LAYERS), :TAPS] = taps[s].astype(F32)


def pair_edges(following, previous):
    sub = lax.broadcasted_iota(jnp.int32, (8, LENGTH), 0)
    return jnp.where(sub < 2, following, jnp.where(sub >= 6, previous, 0.0))


def cluster_edges(following, previous):
    sub = lax.broadcasted_iota(jnp.int32, (8, LENGTH), 0)
    following = pltpu.roll(following, 6, 0)
    previous = pltpu.roll(previous, 2, 0)
    return jnp.where(sub == 0, following, jnp.where(sub == 7, previous, 0.0))


SENT = ((1, 0), (2, 0), (0, 0), (3, 0), (1, 1), (2, 1))


def prepare_kernel(tilt, doses, taps_across, taps_along, pair, clusters, across_bands, down, up, early_even, across, taps, lines):
    wide_taps(taps_across, across)
    lane = lax.broadcasted_iota(jnp.int32, (GROUP, 256), 1)
    group = lax.broadcasted_iota(jnp.int32, (8, 256), 0)
    for z in range(LAYERS):
        offset = ROWS - 8 + ROWS * own_core() + tilt[z]
        for s in range(4):
            line = across[pl.ds(s * LAYERS + z, 1), :]
            wide = jnp.concatenate([line, jnp.zeros_like(line)], 1)
            wide = pltpu.roll(jnp.broadcast_to(wide, (8, 256)), offset, 1)
            band = pltpu.roll(jnp.broadcast_to(wide[:1], (32, 256)), 0, 1, stride=1, stride_axis=0)
            last = jnp.where(group < 2, band[24:], band[:8])
            band = jnp.concatenate([band[8:24], last], 0)
            tail = pltpu.roll(band, 4 * z, 1) if z else band
            tail = jnp.where((lane >= 160 + 4 * z) & (lane < 162 + 4 * z), tail, 0.0)
            across_bands[z, pl.ds(s * GROUP, GROUP), :] = jnp.where(lane < 160, band, tail)
    wide_taps(taps_along, taps)
    lines[...] = jnp.zeros_like(lines)
    for side, (out, near, far) in enumerate(((down, 0, 1), (up, 3, 2))):
        for i, (s, distance) in enumerate(SENT):
            z = far if distance else near
            row = pl.ds(16 * side + 8 + i, 1)
            lines[row, pl.ds(0, 128)] = taps[pl.ds(s * LAYERS + z, 1), :]
            dose = jnp.full((1, 128), doses[s, z], F32)
            for part in range(1, 4):
                rounded = dose.astype(BF16).astype(F32)
                lines[row, pl.ds(128 * part, 128)] = rounded
                dose = dose - rounded
        out[pl.ds(0, 16), :] = pair[tile(near), :]
        out[pl.ds(16, 16), :] = clusters[near]
        out[pl.ds(32, 16), :] = pair[tile(far), :]
        out[pl.ds(48, 16), :] = lines[pl.ds(16 * side, 16), :].astype(BF16)
    odd = lax.rem(lax.axis_index("depth"), 2)

    @pl.when(odd == 0)
    def _():
        early_even[...] = up[pl.ds(0, 48), :]

    @pl.when(odd == 1)
    def _():
        early_even[...] = down[pl.ds(0, 48), :]


def packed_rims(fields):
    sub = lax.broadcasted_iota(jnp.int32, (8, LENGTH), 0)
    total = jnp.where((sub == 0) | (sub == 7), fields[0], 0.0)
    for i, field in enumerate(fields[1:], 1):
        total = jnp.where(sub == i, pltpu.roll(field, i, 0), total)
        total = jnp.where(sub == 7 - i, pltpu.roll(field, 8 - i, 0), total)
    return total


def unpacked_rim(packed, i):
    sub = lax.broadcasted_iota(jnp.int32, (8, LENGTH), 0)
    following = pltpu.roll(packed, 8 - i, 0) if i else packed
    previous = pltpu.roll(packed, i, 0) if i else packed
    return jnp.where(sub == 0, following, jnp.where(sub == 7, previous, 0.0))


def across_kernel(
    mine, near, received, far, corner, bands, early_down, early_up, spread, across_even, across_odd, rims, window
):
    core = own_core()
    payloads = ({}, {})
    for payload, early in zip(payloads, (early_down, early_up)):
        payload[112, 48] = early[pl.ds(0, 48), :]
    for z in range(LAYERS):
        at, also = tile(z), pl.ds(64 + ROWS * z, ROWS)
        parts = [far[0, at, :], far[0, also, :], near[0, at, :], near[0, also, :]]
        parts += [mine[0, at, :], mine[1, at, :], near[1, at, :], near[1, also, :]]
        parts += [far[1, at, :], far[1, also, :], corner[...]]
        for i, part in enumerate(parts):
            window[z, pl.ds(16 * i, 16), :] = part
        x = jnp.dot(bands[z].astype(BF16)[:, :WINDOW], window[z], preferred_element_type=F32)
        spread[z] = x.astype(BF16)
        half = slice(8 * (z // 2), 8 * (z // 2) + 8)
        at = pl.ds(128, 16)
        other = received[at, :].astype(F32)
        following = jnp.where(core == 0, near[1, at, :].astype(F32), other)[half]
        previous = jnp.where(core == 0, other, near[0, at, :].astype(F32))[half]
        if z % 2:
            following = pltpu.roll(following, 4, 0)
        else:
            previous = pltpu.roll(previous, 4, 0)
        rims[0, z] = pair_edges(following, previous)
        rims[1, z] = cluster_edges(following, previous)
        payload = payloads[z // 2]
        own = [x[GROUP * s : GROUP * s + ROWS].astype(BF16) for s in range(4)]
        rim = [x[GROUP * s + ROWS : GROUP * s + GROUP] for s in range(4)]
        if z in (0, 3):
            for i, s in enumerate((1, 2, 0, 3)):
                payload[16 * i, 16] = own[s]
            lines = (early_down if z < 2 else early_up)[pl.ds(48, 16), :].astype(F32)[8:]
            packed = packed_rims((rim[1], rim[2], rims[0, z]))
            payload[64, 16] = jnp.concatenate([packed, lines], 0).astype(BF16)
        else:
            payload[80, 16] = own[1]
            payload[96, 16] = own[2]

    def write(payload, out):
        for (start, size), value in payload.items():
            if start < out.shape[0]:
                out[pl.ds(start, size), :] = value

    odd = lax.rem(lax.axis_index("depth"), 2)

    @pl.when(odd == 0)
    def _():
        write(payloads[0], across_odd)
        write(payloads[1], across_even)

    @pl.when(odd == 1)
    def _():
        write(payloads[0], across_even)
        write(payloads[1], across_odd)


def along_sum(x, matrix):
    rows = x.shape[0]
    zeros = jnp.zeros((rows, 64), F32)
    wide = jnp.concatenate([zeros, x, zeros], 1)
    blocks = LENGTH // 128
    stacked = jnp.concatenate([wide[:, 128 * b : 128 * b + 256] for b in range(blocks)], 0).astype(BF16)
    y = lax.dot_general(stacked, matrix, (((1,), (1,)), ((), ())), preferred_element_type=F32)
    return jnp.concatenate([y[rows * b : rows * (b + 1)] for b in range(blocks)], 1)


def laplace(center, below, above, rows):
    total = center.shape[0]
    inner = center[:rows]
    lane = lax.broadcasted_iota(jnp.int32, (rows, 128), 1)
    right = pltpu.roll(inner, LENGTH - 1, 1)
    left = pltpu.roll(inner, 1, 1)
    right = jnp.concatenate([right[:, :-128], jnp.where(lane == 127, 0.0, right[:, -128:])], 1)
    left = jnp.concatenate([jnp.where(lane == 0, 0.0, left[:, :128]), left[:, 128:]], 1)
    near = right + left
    near = near + pltpu.roll(center, total - 1, 0)[:rows] + pltpu.roll(center, 1, 0)[:rows]
    for layer in (below, above):
        if layer is not None:
            near = near + layer[:rows]
    return near - 6.0 * inner


def substep(spreads, rates, silicon, centers, belows, aboves, arsenic, clusters, rows):
    inter, vacancy, pair = (c[:rows] for c in centers)
    flows = [
        silicon * (spreads[f] * laplace(centers[f], belows[f], aboves[f], rows)) for f in range(3)
    ]
    recombine = rates[0] * inter * vacancy
    pairing = rates[1] * arsenic * inter - rates[2] * pair
    clustering = rates[3] * inter * inter - rates[4] * clusters
    new_inter = inter + (flows[0] - recombine - pairing - 2.0 * clustering)
    new_vacancy = vacancy + (flows[1] - recombine)
    new_pair = pair + (flows[2] + pairing)
    return (new_inter, new_vacancy, new_pair), (arsenic - pairing, clusters + clustering)


NONE = (None, None, None)


def along_kernel(spreads, rates, doses, spread, taps_along, pairs, clusters, rims, outer, late, still, inner, fields, fixed, along):
    wide_taps(taps_along, along)
    for z in range(LAYERS):
        x = spread[z].astype(F32)
        pair = jnp.concatenate([pairs[tile(z), :].astype(F32), rims[0, z]], 0)
        silicon = (pair > 0.0).astype(F32)
        before = jnp.concatenate([clusters[z].astype(F32), rims[1, z]], 0)
        sums = []
        for s in range(4):
            matrix = along_matrix(along[pl.ds(s * LAYERS + z, 1), :])
            y = along_sum(x[GROUP * s : GROUP * (s + 1)], matrix)
            sums.append(doses[s, z] * y)
        fields[0, z] = silicon * sums[1]
        fields[1, z] = silicon * sums[2]
        fields[2, z] = pair
        fixed[0, z] = silicon * sums[0]
        fixed[1, z] = silicon * (before + sums[3])
    for z in range(LAYERS):
        silicon = (fields[2, z] > 0.0).astype(F32)
        belows = [fields[f, z - 1] for f in range(3)] if z > 0 else NONE
        aboves = [fields[f, z + 1] for f in range(3)] if z < LAYERS - 1 else NONE
        centers = [fields[f, z] for f in range(3)]
        mobile, others = substep(spreads, rates, silicon, centers, belows, aboves, fixed[0, z], fixed[1, z], GROUP)
        for f in range(3):
            late[f, z] = mobile[f]
            if z in (0, 3):
                outer[f, z // 3] = fields[f, z, :ROWS]
        for f in range(2):
            still[f, z] = others[f][:ROWS]
    for z in (1, 2):
        silicon = (pairs[tile(z), :].astype(F32) > 0.0).astype(F32)
        centers, belows, aboves = ([late[f, at] for f in range(3)] for at in (z, z - 1, z + 1))
        mobile, others = substep(spreads, rates, silicon, centers, belows, aboves, still[0, z], still[1, z], ROWS)
        for f, new in enumerate((others[0], *mobile, others[1])):
            inner[f, z - 1] = new


def react_kernel(step, spreads, rates, outer, late, still, inner, pairs, rims_own, payload, *refs):
    if step == 0:
        done, near_late, own_late, result, sems = refs
    else:
        early, earlier, result, near_late, own_late, done, sems = refs
    odd = lax.rem(lax.axis_index("depth"), 2)
    side = odd if step == 0 else 1 - odd

    def inward(i):
        return i + side * (3 - 2 * i)

    def copy(half, f, i):
        at = inward(i) if half else 3 - inward(i)
        place = done if half else earlier
        return pltpu.make_async_copy(place.at[f, i], result.at[f, at], sems.at[half, f, i])

    def send(f, i):
        pltpu.make_async_copy(done.at[f, i], result.at[f, inward(i)], sems.at[step, f, i]).start()

    def pairs_of(z):
        return pairs[pl.ds(pl.multiple_of(ROWS * z, ROWS), ROWS), :].astype(F32)

    def sent(i):
        return payload[pl.ds(16 * i, 16), :].astype(F32)

    def known(i):
        return early[pl.ds(16 * i, 16), :].astype(F32) if step else sent(7 + i)

    packed, lines = sent(4)[:8], sent(4)[8:]

    def implanted(i, x):
        line = lines[i : i + 1]
        dose = line[:, 128:129] + line[:, 256:257] + line[:, 384:385]
        return dose * along_sum(x, along_matrix(line[:, :128]))

    pair = jnp.concatenate([known(0), unpacked_rim(packed, 2)], 0)
    silicon = (pair > 0.0).astype(F32)
    near = [
        silicon * implanted(0, jnp.concatenate([sent(0), unpacked_rim(packed, 0)], 0)),
        silicon * implanted(1, jnp.concatenate([sent(1), unpacked_rim(packed, 1)], 0)),
        pair,
    ]
    silicon = silicon[:ROWS]
    arsenic = silicon * implanted(2, sent(2))
    clusters = silicon * (known(1) + implanted(3, sent(3)))
    far_pair = known(2)
    far_silicon = (far_pair > 0.0).astype(F32)
    far = [far_silicon * implanted(4, sent(5)), far_silicon * implanted(5, sent(6)), far_pair]
    beside = [outer[f, side] for f in range(3)]
    z = inward(0)
    own_pair = jnp.concatenate([pairs_of(z), rims_own[0, z]], 0)
    own_silicon = (own_pair > 0.0).astype(F32)
    inner_silicon = (pairs_of(inward(1)) > 0.0).astype(F32)
    for f in range(3):
        change = own_silicon * (spreads[f] * near[f])
        own_late[f] = late[f, z] + change
        done[f + 1, 1] = inner[f + 1, side] + inner_silicon * (spreads[f] * change[:ROWS])
    for f in (0, 4):
        done[f, 1] = inner[f, side]
    for f in range(5):
        send(f, 1)
    mobile, _ = substep(spreads, rates, silicon, near, far, beside, arsenic, clusters, ROWS)
    for f in range(3):
        near_late[f] = mobile[f]
    centers = [own_late[f] for f in range(3)]
    outers = [near_late[f] for f in range(3)]
    inners = [late[f, inward(1)] for f in range(3)]
    mobile, others = substep(
        spreads, rates, own_silicon[:ROWS], centers, outers, inners, still[0, z], still[1, z], ROWS
    )
    for f, new in enumerate((others[0], *mobile, others[1])):
        done[f, 0] = new
        send(f, 0)
    if step == 1:
        for half in range(2):
            for i in range(2):
                for f in range(5):
                    copy(half, f, i).wait()


def both_kernel(*refs):
    given, (from_odd, from_even, early, result) = refs[:8], refs[8:12]
    near_odd, own_odd, near_even, own_even, earlier, done, sems = refs[12:]
    react_kernel(0, *given, from_odd, earlier, near_odd, own_odd, result, sems)
    react_kernel(1, *given, from_even, early, earlier, result, near_even, own_even, done, sems)


def moved(array, axis, size, source):
    route = [(source(i), i) for i in range(size) if source(i) is not None and 0 <= source(i) < size]
    return lax.ppermute(array, axis, route)


def lanes(core0, core1):
    return lambda i: i + core0 if i % 2 == 0 else (None if core1 is None else i + core1)


def body(
    fin_mask,
    stopping_power,
    pairs_before,
    clusters_before,
    taps_across,
    taps_along,
    tilt_shift,
    layer_doses,
    diffusivity,
    reaction_rates,
):
    couples = [[2 * i, 2 * i + 1] for i in range(LATS // 2)]

    def shared(array):
        return lax.all_gather(array, "lat", axis_index_groups=couples)

    core = lax.rem(lax.axis_index("lat"), 2)
    silicon = fin_mask.astype(BF16)
    source = silicon * stopping_power
    pair = silicon * pairs_before
    clusters = silicon * clusters_before
    source, pair, clusters = lax.optimization_barrier((source.reshape(64, LENGTH), pair, clusters))
    mine = shared(source).reshape(128, LENGTH)
    far = moved(mine, "lat", LATS, lanes(-4, 4))
    first = [pair[:, :2], clusters[:, :1], clusters[:, :1]]
    last = [clusters[:, 15:], clusters[:, 15:], pair[:, 14:]]
    first, last = (jnp.concatenate(rows, 1).reshape(16, LENGTH) for rows in (first, last))
    outward, inward = jnp.where(core == 0, first, last), jnp.where(core == 0, last, first)
    pair = pair.reshape(64, LENGTH)
    received = moved(jnp.concatenate([mine, outward], 0), "lat", LATS, lanes(-1, 1))
    corner = jnp.pad(source.reshape(LAYERS, ROWS, LENGTH)[:, :2], ((0, 0), (0, 2), (0, 0))).reshape(16, LENGTH)
    corner = moved(corner, "lat", LATS, lambda i: None if i % 2 == 0 else i + 5)
    across_bands, early_down, early_up, early_even = call(
        prepare_kernel,
        (
            shape((LAYERS, 4 * GROUP, 256), F32),
            shape((64, LENGTH), BF16),
            shape((64, LENGTH), BF16),
            shape((48, LENGTH), BF16),
        ),
        (tilt_shift, layer_doses, taps_across, taps_along, pair, clusters),
        scalars=2,
        scratch=[pltpu.VMEM((16, 128), F32), pltpu.VMEM((16, 128), F32), pltpu.VMEM((32, LENGTH), F32)],
    )
    early_even = moved(early_even, "depth", DEPTHS, lanes(1, -1))
    near = shared(jnp.concatenate([received[:128], inward], 0))
    far, near, early_down, early_up = lax.optimization_barrier((far, near, early_down, early_up))
    far = shared(far)
    spread, to_even, to_odd, rims = call(
        across_kernel,
        (
            shape((LAYERS, 4 * GROUP, LENGTH), BF16),
            shape((112, LENGTH), BF16),
            shape((160, LENGTH), BF16),
            shape((2, LAYERS, 8, LENGTH), F32),
        ),
        (mine.reshape(2, 64, LENGTH), near, received, far, corner, across_bands, early_down, early_up),
        scratch=[pltpu.VMEM((LAYERS, WINDOW, LENGTH), BF16)],
    )
    to_even, to_odd, early_even = lax.optimization_barrier((to_even, to_odd, early_even))
    from_odd = moved(to_odd, "depth", DEPTHS, lanes(-1, 1))
    from_even = moved(to_even, "depth", DEPTHS, lanes(1, -1))
    outer, late, still, inner = call(
        along_kernel,
        (
            shape((3, 2, ROWS, LENGTH), F32),
            shape((3, LAYERS, GROUP, LENGTH), F32),
            shape((2, LAYERS, ROWS, LENGTH), F32),
            shape((5, 2, ROWS, LENGTH), F32),
        ),
        (diffusivity, reaction_rates, layer_doses, spread, taps_along, pair, clusters, rims),
        scalars=3,
        scratch=[
            pltpu.VMEM((3, LAYERS, GROUP, LENGTH), F32),
            pltpu.VMEM((2, LAYERS, GROUP, LENGTH), F32),
            pltpu.VMEM((16, 128), F32),
        ],
    )
    side_scratch = [pltpu.VMEM((3, ROWS, LENGTH), F32), pltpu.VMEM((3, GROUP, LENGTH), F32)]
    half = pltpu.VMEM((5, 2, ROWS, LENGTH), F32)
    return call(
        both_kernel,
        shape((5, LAYERS, ROWS, LENGTH), F32),
        (diffusivity, reaction_rates, outer, late, still, inner, pair, rims, from_odd, from_even, early_even),
        scalars=2,
        hbm_out=True,
        scratch=[*side_scratch, *side_scratch, half, half, pltpu.SemaphoreType.DMA((2, 5, 2))],
    )


def solution(mesh):
    return jax.shard_map(
        body,
        mesh=mesh,
        in_specs=(
            P("depth", "lat", None),
            P("depth", "lat", None),
            P("depth", "lat", None),
            P("depth", "lat", None),
            P(None, "depth", None),
            P(None, "depth", None),
            P("depth"),
            P(None, "depth"),
            P(),
            P(),
        ),
        out_specs=P(None, "depth", "lat", None),
        check_vma=False,
    )
```
